32 devices in a mesh: layer: 4 (over y, x), feat: 8 (over z, core).
Axes of the slice: x: 2, y: 2, z: 4, core: 2. Of those that a mesh axis runs over, the one named last changes fastest.
Arguments:
- activations: bfloat16 [4, 1024, 8192], P(None, None, ('layer', 'feat')), may hold values from -6 to 6
- active_blocks: int32 [4, 1024, 64], P(None, None, ('layer', 'feat')), may hold values from 0 to 1, as said below
- cotangent: bfloat16 [4, 1024, 2048], P(None, 'layer', 'feat'), may hold values from -6 to 6
- decoder: bfloat16 [10, 8192, 2048], P(None, ('layer', 'feat')), may hold values from -0.0625 to 0.0625
Outputs:
- decoder_grad: bfloat16 [10, 8192, 2048], P(None, ('layer', 'feat'))
- feature_grad: bfloat16 [4, 1024, 8192], P(None, None, ('layer', 'feat'))
The draws below stay inside these ranges and needn't reach their ends.
Inputs may be any that keep to these rules, and one draw needn't show every extreme that they name: `active_blocks`: 1 where the block of 128 features is active for that token at that layer, else 0.
All inputs are finite; a program needn't handle non-finite values.
Results may differ from the reference program's by a relative error of at most 0.001.
Values may be sent and summed in bfloat16 or wider, within the bound.
No kernel may reach another device: no remote copies, remote signals or barrier semaphores. Data moves between devices by JAX's collectives and lax.ppermute only.
A program may use at most 128 MiB of HBM per device.

```python
import jax
import jax.numpy as jnp

D = 2048
BLOCK = 128
LAYERS = 4
TOKENS = 1024
PAIRS = 10
F = 8192


def draw_active_blocks(key, part):
    first_key, second_key = jax.random.split(jax.random.fold_in(key, 17))
    levels = jax.random.randint(first_key, (1, 1, F // BLOCK), 1, 6)
    raw_bits = jax.random.randint(second_key, (LAYERS, TOKENS, F // BLOCK), 0, 6)
    return (raw_bits < levels).astype(jnp.int32)


def shard_levels(own_key, shape, shards, low, largest):
    loudness = 1.0
    for axis_at, parts in shards:
        draws = jax.random.uniform(jax.random.fold_in(jax.random.fold_in(own_key, 6), axis_at), (parts,), jnp.float32, low / len(shards), largest / len(shards))
        loudness = loudness * jnp.repeat(jnp.exp(draws), shape[axis_at] // parts).reshape((-1,) + (1,) * (len(shape) - 1 - axis_at))
    return loudness


def noise(key, shape, scale, bound, pieces=(), kind=jnp.bfloat16):
    factor_of = shard_levels(key, shape, pieces, -0.22, 0.18) if pieces else 1.0
    array = jax.random.normal(key, shape, jnp.float32) * scale * factor_of
    return jnp.minimum(jnp.maximum(array, -bound), bound).astype(kind)


def setup_inputs(seed: int = 0) -> dict:
    keys = jax.random.split(jax.random.key(seed), 5)
    return {
        "activations": noise(keys[0], (LAYERS, TOKENS, F), 1.0, 6.0, ((2, 32),)),
        "active_blocks": draw_active_blocks(jax.random.fold_in(keys[4], 71), 0),
        "cotangent": noise(keys[2], (LAYERS, TOKENS, D), 1.0, 6.0, ((1, 4), (2, 8))),
        "decoder": noise(keys[3], (PAIRS, F, D), F ** -0.5, 0.0625, ((1, 32),)),
    }


def reference(activations, active_blocks, cotangent, decoder):
    feature_mask = jnp.repeat(active_blocks, BLOCK, axis=2).astype(jnp.float32)
    sparse = (activations.astype(jnp.float32) * feature_mask).astype(jnp.bfloat16)
    partial_value = jnp.zeros((LAYERS, TOKENS, F), jnp.float32)
    grads = []
    index = 0
    for target in range(LAYERS):
        upstream = cotangent[target]
        for source in range(target + 1):
            grads.append(jnp.dot(sparse[source].T, upstream, preferred_element_type=jnp.float32).astype(jnp.bfloat16))
            term = jnp.dot(upstream, decoder[index].T, preferred_element_type=jnp.float32)
            partial_value = partial_value.at[source].add(term)
            index = index + 1
    return jnp.stack(grads), (partial_value * feature_mask).astype(jnp.bfloat16)
```

```python
import jax
import jax.numpy as jnp
from jax import lax
from jax.sharding import PartitionSpec as P


def body(activations, active_blocks, cotangent, decoder):
    width = activations.shape[2] // active_blocks.shape[2]
    layers = activations.shape[0]
    feature_mask = jnp.repeat(active_blocks, width, axis=2).astype(jnp.float32)
    sparse = (activations.astype(jnp.float32) * feature_mask).astype(jnp.bfloat16)
    n_layer = lax.axis_size("layer")
    n_feat = lax.axis_size("feat")
    blocks = lax.all_gather(cotangent, ("layer", "feat"), axis=0, tiled=False)
    g, t, d = cotangent.shape
    upstream = blocks.reshape(n_layer, n_feat, g, t, d).transpose(2, 0, 3, 1, 4)
    upstream = upstream.reshape(g, n_layer * t, n_feat * d)
    grads = []
    total = jnp.zeros((layers, sparse.shape[1], sparse.shape[2]), jnp.float32)
    offset = 0
    for target in range(layers):
        count = target + 1
        rows = decoder[offset : offset + count]
        grads.append(
            jnp.einsum("stf,td->sfd", sparse[:count], upstream[target], preferred_element_type=jnp.float32).astype(jnp.bfloat16)
        )
        total = total.at[:count].add(
            jnp.einsum("td,sfd->stf", upstream[target], rows, preferred_element_type=jnp.float32)
        )
        offset = offset + count
    return jnp.concatenate(grads, axis=0), (total * feature_mask).astype(jnp.bfloat16)


def solution(mesh):
    in_specs = (
        P(None, None, ("layer", "feat")),
        P(None, None, ("layer", "feat")),
        P(None, "layer", "feat"),
        P(None, ("layer", "feat"), None),
    )
    out_specs = (P(None, ("layer", "feat"), None), P(None, None, ("layer", "feat")))
    return jax.shard_map(body, mesh=mesh, in_specs=in_specs, out_specs=out_specs, check_vma=False)
```

```python
import functools

import jax
import jax.numpy as jnp
from jax import lax
from jax.experimental import pallas as pl
from jax.experimental.pallas import tpu as pltpu
from jax.sharding import PartitionSpec as P

CORES = 2


def plane_order(planes):
    return [
        sorted(range(planes), key=lambda p: (abs(p - z), p != (z ^ 1))) for z in range(planes)
    ]


def line_groups(order):
    groups = {}
    for z, row in enumerate(order):
        for r in range(1, len(row)):
            step = 1 if row[r] > z else -1
            held = order[z + step].index(row[r])
            key = (abs(row[r] - z), r, held)
            groups.setdefault(key, []).append((z + step, z))
    return [(r, held, groups[(dist, r, held)]) for dist, r, held in sorted(groups)]


class Gather:
    def __init__(self, block, n_layer, n_feat):
        self.n_layer, self.n_feat = n_layer, n_feat
        self.planes = n_feat // CORES
        self.targets = block.shape[0]
        self.order = plane_order(self.planes)
        self.plane = lax.axis_index("feat") // CORES
        groups = line_groups(self.order)
        self.pieces = {(0, 0): [(0, block)]}
        self.along_line(groups, 0, range(1, self.planes))
        far = [0] + ([self.planes - 1] if self.planes > 1 else [])
        near = [r for r in range(self.planes) if r not in far]
        singles = [j for j in range(1, n_layer) if j & (j - 1) == 0]
        others = [j for j in range(1, n_layer) if j & (j - 1) != 0]
        for r in range(self.planes):
            for j in singles:
                self.pieces[(r, j)] = self.across(self.pieces[(r, 0)], j)
            if r in far:
                for j in others:
                    self.diagonal(r, j)
        for j in others:
            self.along_line(groups, j, near)
        self.other = {
            key: [(g, self.swap(x)) for g, x in parts] for key, parts in self.pieces.items()
        }

    def permute(self, x, pairs):
        flat = []
        for (l0, f0), (l1, f1) in pairs:
            flat.append((l0 * self.n_feat + f0, l1 * self.n_feat + f1))
        return lax.ppermute(x, ("layer", "feat"), sorted(flat))

    def swap(self, x):
        return self.permute(
            x,
            [((l, f), (l, f ^ 1)) for l in range(self.n_layer) for f in range(self.n_feat)],
        )

    def across_one(self, x, bit):
        return self.permute(
            x,
            [((l, f), (l ^ bit, f)) for l in range(self.n_layer) for f in range(self.n_feat)],
        )

    def across(self, parts, bit):
        return [(g, self.across_one(x, bit)) for g, x in parts]

    def diagonal(self, r, j):
        bits = [1 << b for b in range(j.bit_length()) if j >> b & 1]
        if len(bits) == 2 and self.targets % 2 == 0:
            half = self.targets // 2
            out = []
            for at, bit in enumerate(bits):
                (_, x), = self.pieces[(r, j ^ bit)]
                part = lax.slice_in_dim(x, at * half, (at + 1) * half, axis=0)
                out.append((at * half, self.across_one(part, bit)))
            self.pieces[(r, j)] = out
        else:
            self.pieces[(r, j)] = self.across(self.pieces[(r, j ^ bits[0])], bits[0])

    def along_line(self, groups, j, rounds):
        for r, held, moves in groups:
            if r not in rounds:
                continue
            pairs = [
                ((l, a * CORES + c), (l, b * CORES + c))
                for l in range(self.n_layer)
                for a, b in moves
                for c in range(CORES)
            ]
            got = [(g, self.permute(x, pairs)) for g, x in self.pieces[(held, j)]]
            if (r, j) in self.pieces:
                here = functools.reduce(jnp.logical_or, [self.plane == b for _, b in moves])
                got = [
                    (g, jnp.where(here, new, old))
                    for (g, new), (_, old) in zip(got, self.pieces[(r, j)])
                ]
            self.pieces[(r, j)] = got


def round_kernel(layout, layers, first, last, meta, sparse, decoder, *refs):
    n_parts = len(layout)
    refs = list(refs)
    mask = refs.pop(0) if last else None
    acc_in = None if first else refs.pop(0)
    parts = [refs[:n_parts], refs[n_parts : 2 * n_parts]]
    refs = refs[2 * n_parts :]
    if not first:
        refs.pop(0)
    grad, acc_out = refs[:2]
    up_v, sparse_v, dec_v, acc_v, grad_v, feat_v, part_sem, in_sem, out_sem = refs[2:]
    tokens, wide = parts[0][0].shape[1:]
    pairs = decoder.shape[0]

    def columns(k):
        return pl.ds(pl.multiple_of(meta[k] * wide, wide), wide)

    def load_parts(k):
        out = []
        for i, (j, g, count) in enumerate(layout):
            rows = pl.ds(pl.multiple_of(meta[2 + j] * tokens, tokens), tokens)
            out.append(
                pltpu.make_async_copy(
                    parts[k][i], up_v.at[k, pl.ds(g, count), rows, :], part_sem.at[k, i]
                )
            )
        return out

    part_copies = [load_parts(0), load_parts(1)]
    dec_copies = [
        pltpu.make_async_copy(decoder.at[:, :, columns(k)], dec_v.at[k], in_sem.at[k]) for k in range(2)
    ]
    sparse_copy = pltpu.make_async_copy(sparse, sparse_v, in_sem.at[2])
    sparse_copy.start()
    for c in part_copies[0]:
        c.start()
    dec_copies[0].start()
    acc_copy = None
    if not first:
        acc_copy = pltpu.make_async_copy(acc_in, acc_v, in_sem.at[3])
        acc_copy.start()
    for c in part_copies[1]:
        c.start()
    dec_copies[1].start()
    mask_copy = None
    if last:
        mask_copy = pltpu.make_async_copy(mask, feat_v, in_sem.at[4])
        mask_copy.start()
    outs = []

    def grads(k):
        for target in range(layers):
            base = target * (target + 1) // 2

            @pl.loop(0, target + 1)
            def _(source):
                grad_v[k, base + source] = jnp.dot(
                    sparse_v[source], up_v[k, target], preferred_element_type=jnp.float32
                ).astype(jnp.bfloat16)

        out = pltpu.make_async_copy(grad_v.at[k], grad.at[:, :, columns(k)], out_sem.at[k])
        out.start()
        outs.append(out)

    def features(k, final):
        for source in range(layers):
            if k == 0 and first:
                acc_v[source] = jnp.zeros(acc_v.shape[1:], jnp.float32)

            @pl.loop(source, layers)
            def _(target):
                pair = target * (target + 1) // 2 + source
                acc_v[source] += lax.dot_general(
                    up_v[k, target],
                    dec_v[k, pair],
                    (((1,), (1,)), ((), ())),
                    preferred_element_type=jnp.float32,
                )

            if final:
                if last:
                    feat_v[source] = (acc_v[source] * feat_v[source].astype(jnp.float32)).astype(
                        jnp.bfloat16
                    )
                out = pltpu.make_async_copy(
                    (feat_v if last else acc_v).at[source], acc_out.at[source], out_sem.at[2 + source]
                )
                out.start()
                outs.append(out)

    sparse_copy.wait()
    for c in part_copies[0]:
        c.wait()
    grads(0)
    dec_copies[0].wait()
    if acc_copy is not None:
        acc_copy.wait()
    features(0, False)
    for c in part_copies[1]:
        c.wait()
    grads(1)
    dec_copies[1].wait()
    if mask_copy is not None:
        mask_copy.wait()
    features(1, True)
    for out in outs:
        out.wait()


def run_round(meta, sparse, decoder, mask, acc, grad, mine, theirs, last):
    first = acc is None
    layers, width, tokens = sparse.shape
    layout = [(j, g, x.shape[0]) for j, part in mine for g, x in part]
    arrays = [x for _, part in mine for _, x in part] + [x for _, part in theirs for _, x in part]
    wide = arrays[0].shape[2]
    pairs = decoder.shape[0]
    operands = [meta, sparse, decoder]
    if last:
        operands.append(mask)
    if not first:
        operands.append(acc)
    operands += arrays
    aliases = {}
    if not first:
        aliases[len(operands)] = 0
        operands.append(grad)
    specs = [pl.BlockSpec(memory_space=pltpu.SMEM)] + [pl.BlockSpec(memory_space=pl.ANY)] * (
        len(operands) - 1
    )
    flops = 2 * 2 * 2 * pairs * width * tokens * wide
    return pl.pallas_call(
        functools.partial(round_kernel, layout, layers, first, last),
        out_shape=(
            jax.ShapeDtypeStruct(decoder.shape, jnp.bfloat16),
            jax.ShapeDtypeStruct((layers, tokens, width), jnp.bfloat16 if last else jnp.float32),
        ),
        in_specs=specs,
        out_specs=(pl.BlockSpec(memory_space=pl.ANY), pl.BlockSpec(memory_space=pl.ANY)),
        scratch_shapes=[
            pltpu.VMEM((2, layers, tokens, wide), jnp.bfloat16),
            pltpu.VMEM((layers, width, tokens), jnp.bfloat16),
            pltpu.VMEM((2, pairs, width, wide), jnp.bfloat16),
            pltpu.VMEM((layers, tokens, width), jnp.float32),
            pltpu.VMEM((2, pairs, width, wide), jnp.bfloat16),
            pltpu.VMEM((layers, tokens, width), jnp.bfloat16),
            pltpu.SemaphoreType.DMA((2, len(layout))),
            pltpu.SemaphoreType.DMA((5,)),
            pltpu.SemaphoreType.DMA((2 + layers,)),
        ],
        input_output_aliases=aliases,
        cost_estimate=pl.CostEstimate(flops=flops, bytes_accessed=20 * 2**20, transcendentals=0),
        compiler_params=pltpu.CompilerParams(vmem_limit_bytes=40 * 2**20),
    )(*operands)


def body(n_layer, n_feat, activations, active_blocks, cotangent, decoder):
    width = activations.shape[2] // active_blocks.shape[2]
    feature_mask = jnp.repeat(active_blocks, width, axis=2).astype(jnp.bfloat16)
    sparse = jnp.swapaxes(activations * feature_mask, 1, 2)
    blocks = Gather(cotangent, n_layer, n_feat)
    core = lax.axis_index("feat") % CORES
    rows = [lax.axis_index("layer") ^ j for j in range(n_layer)]
    acc = grad = None
    for r in range(blocks.planes):
        plane = jnp.asarray([row[r] for row in blocks.order], jnp.int32)[blocks.plane]
        meta = jnp.stack([plane * CORES + core, plane * CORES + 1 - core] + rows).astype(jnp.int32)
        mine = [(j, blocks.pieces[(r, j)]) for j in range(n_layer)]
        theirs = [(j, blocks.other[(r, j)]) for j in range(n_layer)]
        grad, acc = run_round(
            meta, sparse, decoder, feature_mask, acc, grad, mine, theirs, r == blocks.planes - 1
        )
    return grad, acc


def solution(mesh):
    in_specs = (
        P(None, None, ("layer", "feat")),
        P(None, None, ("layer", "feat")),
        P(None, "layer", "feat"),
        P(None, ("layer", "feat"), None),
    )
    out_specs = (P(None, ("layer", "feat"), None), P(None, None, ("layer", "feat")))
    work = functools.partial(body, mesh.shape["layer"], mesh.shape["feat"])
    return jax.shard_map(work, mesh=mesh, in_specs=in_specs, out_specs=out_specs, check_vma=False)
```

```python
import functools

import jax
import jax.numpy as jnp
from jax import lax
from jax.experimental import pallas as pl
from jax.experimental.pallas import tpu as pltpu
from jax.sharding import Mesh
from jax.sharding import PartitionSpec as P

CORES = 2


def target_kernel(target, layers, core, sparse, decoder, mask, mine, theirs, *refs):
    refs = list(refs)
    top = target == layers - 1
    acc_in = None if top else refs.pop(0)
    if not top:
        refs = refs[2:]
    grad, feat = refs[:2]
    acc_out = refs[2] if target > 0 else None
    refs = refs[3:] if target > 0 else refs[2:]
    up_v, sparse_v, dec_v, mask_v, acc_v, grad_v, feat_v, up_sem, in_sem, grad_sem, out_sem = refs
    count = target + 1
    base = target * (target + 1) // 2
    n_layer, n_plane, tokens, wide = mine.shape
    width = sparse.shape[1]
    depth = n_plane * CORES * wide
    rows = n_layer * tokens

    def columns(plane, which):
        at = core[0] if which == 0 else 1 - core[0]
        return pl.ds(pl.multiple_of((plane * CORES + at) * wide, wide), wide)

    sparse_copy = pltpu.make_async_copy(sparse.at[pl.ds(0, count)], sparse_v, in_sem.at[0])
    sparse_copy.start()
    ups = []
    for which, ref in enumerate((mine, theirs)):
        for plane in range(n_plane):
            copy = pltpu.make_async_copy(
                ref.at[:, plane], up_v.at[:, :, columns(plane, which)], up_sem.at[which, plane]
            )
            copy.start()
            ups.append((copy, plane, which))
    dec_copy = pltpu.make_async_copy(decoder, dec_v, in_sem.at[1])
    dec_copy.start()
    acc_copy = None
    if not top:
        acc_copy = pltpu.make_async_copy(acc_in.at[pl.ds(0, count)], acc_v, in_sem.at[2])
        acc_copy.start()
    mask_copy = pltpu.make_async_copy(mask.at[target], mask_v, in_sem.at[3])
    mask_copy.start()
    sparse_copy.wait()
    outs = []
    for at, (copy, plane, which) in enumerate(ups):
        copy.wait()
        cols = columns(plane, which)
        grad_v[:, :, cols] = (
            jnp.dot(
                sparse_v[...].reshape(count * width, rows),
                up_v[:, :, cols].reshape(rows, wide),
                preferred_element_type=jnp.float32,
            )
            .astype(jnp.bfloat16)
            .reshape(count, width, wide)
        )
        out = pltpu.make_async_copy(
            grad_v.at[:, :, cols], grad.at[pl.ds(base, count), :, cols], grad_sem.at[at]
        )
        out.start()
        outs.append(out)
    dec_copy.wait()
    mask_copy.wait()
    if acc_copy is not None:
        acc_copy.wait()
    for source in reversed(range(count)):
        total = jnp.dot(
            up_v[...].reshape(rows, depth), dec_v[source], preferred_element_type=jnp.float32
        )
        if not top:
            total = acc_v[source] + total
        if source == target:
            feat_v[...] = (total * mask_v[...].astype(jnp.float32)).astype(jnp.bfloat16)
            out = pltpu.make_async_copy(feat_v, feat.at[source], out_sem.at[source])
        else:
            acc_v[source] = total
            out = pltpu.make_async_copy(acc_v.at[source], acc_out.at[source], out_sem.at[source])
        out.start()
        outs.append(out)
    for out in outs:
        out.wait()


def run_target(target, core, sparse, decoder, pairs, mask, mine, theirs, acc, grad, feat):
    top = acc is None
    layers, width, rows = sparse.shape
    n_layer, n_plane, tokens, wide = mine.shape
    depth = n_plane * CORES * wide
    count = target + 1
    operands = [core, sparse, decoder, mask, mine, theirs]
    aliases = {}
    if not top:
        operands += [acc, grad, feat]
        aliases = {7: 0, 8: 1}
    any_space = pl.BlockSpec(memory_space=pl.ANY)
    out_shape = [
        jax.ShapeDtypeStruct((pairs, width, depth), jnp.bfloat16),
        jax.ShapeDtypeStruct((layers, rows, width), jnp.bfloat16),
    ]
    if target > 0:
        out_shape.append(jax.ShapeDtypeStruct((target, rows, width), jnp.float32))
    flops = 4 * count * width * rows * depth
    outs = pl.pallas_call(
        functools.partial(target_kernel, target, layers),
        out_shape=tuple(out_shape),
        in_specs=[pl.BlockSpec(memory_space=pltpu.SMEM)] + [any_space] * (len(operands) - 1),
        out_specs=tuple([any_space] * len(out_shape)),
        scratch_shapes=[
            pltpu.VMEM((n_layer, tokens, depth), jnp.bfloat16),
            pltpu.VMEM((count, width, rows), jnp.bfloat16),
            pltpu.VMEM((count, depth, width), jnp.bfloat16),
            pltpu.VMEM((rows, width), jnp.bfloat16),
            pltpu.VMEM((count, rows, width), jnp.float32),
            pltpu.VMEM((count, width, depth), jnp.bfloat16),
            pltpu.VMEM((rows, width), jnp.bfloat16),
            pltpu.SemaphoreType.DMA((CORES, n_plane)),
            pltpu.SemaphoreType.DMA((4,)),
            pltpu.SemaphoreType.DMA((CORES * n_plane,)),
            pltpu.SemaphoreType.DMA((count,)),
        ],
        input_output_aliases=aliases,
        cost_estimate=pl.CostEstimate(flops=flops, bytes_accessed=12 * 2**20, transcendentals=0),
        compiler_params=pltpu.CompilerParams(vmem_limit_bytes=44 * 2**20),
    )(*operands)
    return outs if target > 0 else (*outs, None)


def body(activations, active_blocks, cotangent, decoder):
    width = activations.shape[2] // active_blocks.shape[2]
    layers = cotangent.shape[0]
    order = list(reversed(range(layers)))
    blocks = {
        target: lax.all_gather(cotangent[target], ("layer", "plane"), axis=0, tiled=False)
        for target in order
    }
    turned = jnp.repeat(jnp.swapaxes(active_blocks, 1, 2).astype(jnp.bfloat16), width, axis=1)
    sparse = jnp.swapaxes(activations, 1, 2) * turned
    mask = jnp.swapaxes(turned, 1, 2)
    rows = {}
    for target in order:
        base = target * (target + 1) // 2
        rows[target] = jnp.swapaxes(decoder[base : base + target + 1], 1, 2)
    core = lax.axis_index("core").astype(jnp.int32).reshape(1)
    acc = grad = feat = None
    ready = (sparse, mask, [rows[target] for target in order])
    for target in order:
        mine, ready = lax.optimization_barrier((blocks[target], ready))
        if grad is None:
            sparse, mask, turned_rows = ready
            rows = dict(zip(order, turned_rows))
        else:
            grad, feat, acc = ready
        mine = mine.reshape(lax.axis_size("layer"), lax.axis_size("plane"), *mine.shape[1:])
        theirs = lax.ppermute(mine, "core", [(c, c ^ 1) for c in range(CORES)])
        grad, feat, acc = run_target(
            target, core, sparse, rows[target], decoder.shape[0], mask, mine, theirs, acc, grad, feat
        )
        ready = (grad, feat, acc)
    return grad, feat


def solution(mesh):
    n_layer, n_feat = mesh.devices.shape
    fine = Mesh(
        mesh.devices.reshape(n_layer, n_feat // CORES, CORES), ("layer", "plane", "core")
    )
    every = ("layer", "plane", "core")
    in_specs = (
        P(None, None, every),
        P(None, None, every),
        P(None, "layer", ("plane", "core")),
        P(None, every, None),
    )
    out_specs = (P(None, every, None), P(None, None, every))
    return jax.shard_map(body, mesh=fine, in_specs=in_specs, out_specs=out_specs, check_vma=False)
```

```python
import functools

import jax
import jax.numpy as jnp
from jax import lax
from jax.experimental import pallas as pl
from jax.experimental.pallas import tpu as pltpu
from jax.sharding import PartitionSpec as P


def target_kernel(target, layers, sparse, decoder, mask, mine, *refs):
    refs = list(refs)
    top = target == layers - 1
    acc_in = None if top else refs.pop(0)
    if not top:
        refs = refs[2:]
    grad, feat = refs[:2]
    acc_out = refs[2] if target > 0 else None
    refs = refs[3:] if target > 0 else refs[2:]
    up_v, sparse_v, dec_v, mask_v, acc_v, grad_v, feat_v, up_sem, in_sem, grad_sem, out_sem = refs
    count = target + 1
    base = target * (target + 1) // 2
    n_layer, n_feat, tokens, wide = mine.shape
    width = sparse.shape[1]
    depth = n_feat * wide
    rows = n_layer * tokens

    def columns(at):
        return pl.ds(at * wide, wide)

    sparse_copy = pltpu.make_async_copy(sparse.at[pl.ds(0, count)], sparse_v, in_sem.at[0])
    sparse_copy.start()
    ups = [
        pltpu.make_async_copy(mine.at[:, at], up_v.at[:, :, columns(at)], up_sem.at[at])
        for at in range(n_feat)
    ]
    for copy in ups:
        copy.start()
    dec_copy = pltpu.make_async_copy(decoder, dec_v, in_sem.at[1])
    dec_copy.start()
    acc_copy = None
    if not top:
        acc_copy = pltpu.make_async_copy(acc_in.at[pl.ds(0, count)], acc_v, in_sem.at[2])
        acc_copy.start()
    mask_copy = pltpu.make_async_copy(mask.at[target], mask_v, in_sem.at[3])
    mask_copy.start()
    sparse_copy.wait()
    outs = []
    for at, copy in enumerate(ups):
        copy.wait()
        cols = columns(at)
        grad_v[:, :, cols] = (
            jnp.dot(
                sparse_v[...].reshape(count * width, rows),
                up_v[:, :, cols].reshape(rows, wide),
                preferred_element_type=jnp.float32,
            )
            .astype(jnp.bfloat16)
            .reshape(count, width, wide)
        )
        out = pltpu.make_async_copy(
            grad_v.at[:, :, cols], grad.at[pl.ds(base, count), :, cols], grad_sem.at[at]
        )
        out.start()
        outs.append(out)
    dec_copy.wait()
    mask_copy.wait()
    if acc_copy is not None:
        acc_copy.wait()
    for source in reversed(range(count)):
        total = jnp.dot(
            up_v[...].reshape(rows, depth), dec_v[source], preferred_element_type=jnp.float32
        )
        if not top:
            total = acc_v[source] + total
        if source == target:
            feat_v[...] = (total * mask_v[...].astype(jnp.float32)).astype(jnp.bfloat16)
            out = pltpu.make_async_copy(feat_v, feat.at[source], out_sem.at[source])
        else:
            acc_v[source] = total
            out = pltpu.make_async_copy(acc_v.at[source], acc_out.at[source], out_sem.at[source])
        out.start()
        outs.append(out)
    for out in outs:
        out.wait()


def run_target(target, sparse, decoder, pairs, mask, mine, acc, grad, feat):
    top = acc is None
    layers, width, rows = sparse.shape
    n_layer, n_feat, tokens, wide = mine.shape
    depth = n_feat * wide
    count = target + 1
    operands = [sparse, decoder, mask, mine]
    aliases = {}
    if not top:
        operands += [acc, grad, feat]
        aliases = {5: 0, 6: 1}
    any_space = pl.BlockSpec(memory_space=pl.ANY)
    out_shape = [
        jax.ShapeDtypeStruct((pairs, width, depth), jnp.bfloat16),
        jax.ShapeDtypeStruct((layers, rows, width), jnp.bfloat16),
    ]
    if target > 0:
        out_shape.append(jax.ShapeDtypeStruct((target, rows, width), jnp.float32))
    flops = 4 * count * width * rows * depth
    outs = pl.pallas_call(
        functools.partial(target_kernel, target, layers),
        out_shape=tuple(out_shape),
        in_specs=[any_space] * len(operands),
        out_specs=tuple([any_space] * len(out_shape)),
        scratch_shapes=[
            pltpu.VMEM((n_layer, tokens, depth), jnp.bfloat16),
            pltpu.VMEM((count, width, rows), jnp.bfloat16),
            pltpu.VMEM((count, depth, width), jnp.bfloat16),
            pltpu.VMEM((rows, width), jnp.bfloat16),
            pltpu.VMEM((count, rows, width), jnp.float32),
            pltpu.VMEM((count, width, depth), jnp.bfloat16),
            pltpu.VMEM((rows, width), jnp.bfloat16),
            pltpu.SemaphoreType.DMA((n_feat,)),
            pltpu.SemaphoreType.DMA((4,)),
            pltpu.SemaphoreType.DMA((n_feat,)),
            pltpu.SemaphoreType.DMA((count,)),
        ],
        input_output_aliases=aliases,
        cost_estimate=pl.CostEstimate(flops=flops, bytes_accessed=12 * 2**20, transcendentals=0),
        compiler_params=pltpu.CompilerParams(vmem_limit_bytes=44 * 2**20),
    )(*operands)
    return outs if target > 0 else (*outs, None)


def body(activations, active_blocks, cotangent, decoder):
    width = activations.shape[2] // active_blocks.shape[2]
    layers = cotangent.shape[0]
    order = list(reversed(range(layers)))
    blocks = {
        target: lax.all_gather(cotangent[target], ("layer", "feat"), axis=0, tiled=False)
        for target in order
    }
    turned = jnp.repeat(jnp.swapaxes(active_blocks, 1, 2).astype(jnp.bfloat16), width, axis=1)
    sparse = jnp.swapaxes(activations, 1, 2) * turned
    mask = jnp.swapaxes(turned, 1, 2)
    rows = {}
    for target in order:
        base = target * (target + 1) // 2
        rows[target] = jnp.swapaxes(decoder[base : base + target + 1], 1, 2)
    acc = grad = feat = None
    ready = (sparse, mask, [rows[target] for target in order])
    for target in order:
        mine, ready = lax.optimization_barrier((blocks[target], ready))
        if grad is None:
            sparse, mask, turned_rows = ready
            rows = dict(zip(order, turned_rows))
        else:
            grad, feat, acc = ready
        mine = mine.reshape(lax.axis_size("layer"), lax.axis_size("feat"), *mine.shape[1:])
        grad, feat, acc = run_target(
            target, sparse, rows[target], decoder.shape[0], mask, mine, acc, grad, feat
        )
        ready = (grad, feat, acc)
    return grad, feat


def solution(mesh):
    in_specs = (
        P(None, None, ("layer", "feat")),
        P(None, None, ("layer", "feat")),
        P(None, "layer", "feat"),
        P(None, ("layer", "feat"), None),
    )
    out_specs = (P(None, ("layer", "feat"), None), P(None, None, ("layer", "feat")))
    return jax.shard_map(body, mesh=mesh, in_specs=in_specs, out_specs=out_specs, check_vma=False)
```

```python
import functools

import jax
import jax.numpy as jnp
from jax import lax
from jax.experimental import pallas as pl
from jax.experimental.pallas import tpu as pltpu
from jax.sharding import PartitionSpec as P

CORES = 2
VMEM_LIMIT = 60 * 2**20


def plane_order(planes):
    return [
        sorted(range(planes), key=lambda p: (abs(p - z), p != (z ^ 1))) for z in range(planes)
    ]


def line_groups(order):
    groups = {}
    for z, row in enumerate(order):
        for r in range(1, len(row)):
            step = 1 if row[r] > z else -1
            held = order[z + step].index(row[r])
            groups.setdefault((abs(row[r] - z), r, held), []).append((z + step, z))
    return [(*key, groups[key]) for key in sorted(groups)]


class Gather:
    def __init__(self, block, n_layer, n_feat):
        self.n_layer, self.n_feat = n_layer, n_feat
        self.planes = n_feat // CORES
        self.order = plane_order(self.planes)
        self.plane = lax.axis_index("feat") // CORES
        self.groups = line_groups(self.order)
        self.singles = [j for j in range(1, n_layer) if j & (j - 1) == 0]
        self.others = [j for j in range(1, n_layer) if j & (j - 1) != 0]
        self.pieces = {(0, 0): block}
        self.sent = []
        self.token = None

    def tie(self, x):
        if self.token is None:
            return x
        return lax.optimization_barrier((x, self.token))[0]

    def permute(self, x, pairs):
        flat = [(l0 * self.n_feat + f0, l1 * self.n_feat + f1) for (l0, f0), (l1, f1) in pairs]
        return lax.ppermute(x, ("layer", "feat"), sorted(flat))

    def swap(self, x):
        every = [(l, f) for l in range(self.n_layer) for f in range(self.n_feat)]
        return self.permute(x, [((l, f), (l, f ^ 1)) for l, f in every])

    def across(self, r, j, bit):
        every = [(l, f) for l in range(self.n_layer) for f in range(self.n_feat)]
        x = self.tie(self.pieces[(r, j ^ bit)])
        self.sent.append(x)
        self.pieces[(r, j)] = self.permute(x, [((l, f), (l ^ bit, f)) for l, f in every])

    def straight(self, r):
        for j in self.singles:
            self.across(r, j, j)

    def diagonal(self, r):
        for j in self.others:
            bits = [1 << b for b in range(j.bit_length()) if j >> b & 1]
            self.across(r, j, bits[0] if r == 0 else bits[-1])

    def along_line(self, j, rounds, hops):
        for dist, r, held, moves in self.groups:
            if r not in rounds or dist not in hops:
                continue
            pairs = [
                ((l, a * CORES + c), (l, b * CORES + c))
                for l in range(self.n_layer)
                for a, b in moves
                for c in range(CORES)
            ]
            x = self.tie(self.pieces[(held, j)])
            self.sent.append(x)
            got = self.permute(x, pairs)
            if (r, j) in self.pieces:
                here = functools.reduce(jnp.logical_or, [self.plane == b for _, b in moves])
                got = jnp.where(here, got, self.pieces[(r, j)])
            self.pieces[(r, j)] = got


def prepare_kernel(act, blocks, sparse, mask):
    width, rows = sparse.shape[1:]
    count = blocks.shape[1]
    bits = blocks[0].astype(jnp.float32)
    turned = jnp.concatenate(
        [jnp.broadcast_to(bits[b : b + 1], (width // count, rows)) for b in range(count)], axis=0
    ).astype(jnp.bfloat16)
    sparse[0] = act[0].T * turned
    mask[0] = turned.T


def prepare(activations, active_blocks):
    layers, rows, width = activations.shape
    count = active_blocks.shape[2]

    def block(*shape):
        return pl.BlockSpec((1, *shape), lambda s: (s, 0, 0))

    return pl.pallas_call(
        prepare_kernel,
        grid=(layers,),
        in_specs=[block(rows, width), block(count, rows)],
        out_specs=(block(width, rows), block(rows, width)),
        out_shape=(
            jax.ShapeDtypeStruct((layers, width, rows), jnp.bfloat16),
            jax.ShapeDtypeStruct((layers, rows, width), jnp.bfloat16),
        ),
        cost_estimate=pl.CostEstimate(flops=0, bytes_accessed=6 * layers * rows * width, transcendentals=0),
        compiler_params=pltpu.CompilerParams(vmem_limit_bytes=VMEM_LIMIT),
    )(activations, jnp.swapaxes(active_blocks, 1, 2))


def round_kernel(n_layer, layers, first, last, meta, sparse, decoder, *refs):
    refs = list(refs)
    mask = refs.pop(0) if last else None
    acc_in = None if first else refs.pop(0)
    parts = refs[: CORES * n_layer]
    refs = refs[CORES * n_layer :]
    if not first:
        refs.pop(0)
    grad, acc_out, token = refs[:3]
    up_v, sparse_v, dec_v, acc_v, grad_v, feat_v, up_sem, dec_sem, in_sem, grad_sem, out_sem = refs[3:]
    tokens, wide = parts[0].shape[1:]
    both = CORES * wide
    width = decoder.shape[1]
    rows = n_layer * tokens
    columns = pl.ds(pl.multiple_of(meta[0] * both, both), both)
    token[...] = jnp.zeros_like(token)

    copies = [pltpu.make_async_copy(sparse, sparse_v, in_sem.at[0])]
    ups = {}
    for target in range(layers):
        ups[target] = []
        for i, part in enumerate(parts):
            core = meta[1] if i < n_layer else 1 - meta[1]
            at_rows = pl.ds(pl.multiple_of(meta[2 + i % n_layer] * tokens, tokens), tokens)
            at_cols = pl.ds(pl.multiple_of(target * both + core * wide, wide), wide)
            ups[target].append(
                pltpu.make_async_copy(
                    part.at[target], up_v.at[at_rows, at_cols], up_sem.at[target, i]
                )
            )
    decs = []
    for target in range(layers):
        for source in range(target + 1):
            pair = target * (target + 1) // 2 + source
            decs.append(
                pltpu.make_async_copy(
                    decoder.at[pair, :, columns],
                    dec_v.at[source, :, pl.ds(target * both, both)],
                    dec_sem.at[pair],
                )
            )
    copies[0].start()
    for target in reversed(range(layers)):
        for copy in ups[target]:
            copy.start()
    for copy in decs:
        copy.start()
    acc_copies = []
    if not first:
        for source in range(layers):
            acc_copies.append(
                pltpu.make_async_copy(acc_in.at[source], acc_v.at[source], in_sem.at[2 + source])
            )
            acc_copies[-1].start()
    if last:
        mask_copy = pltpu.make_async_copy(mask, feat_v, in_sem.at[1])
        mask_copy.start()
    copies[0].wait()
    outs = []
    for target in reversed(range(layers)):
        for copy in ups[target]:
            copy.wait()
        count = target + 1
        base = target * (target + 1) // 2
        for core in range(CORES):
            grad_v[pl.ds(base, count), :, core * wide : (core + 1) * wide] = (
                jnp.dot(
                    sparse_v[:count].reshape(count * width, rows),
                    up_v[:, target * both + core * wide : target * both + (core + 1) * wide],
                    preferred_element_type=jnp.float32,
                )
                .astype(jnp.bfloat16)
                .reshape(count, width, wide)
            )
        out = pltpu.make_async_copy(
            grad_v.at[pl.ds(base, count)], grad.at[pl.ds(base, count), :, columns], grad_sem.at[target]
        )
        out.start()
        outs.append(out)
    for copy in decs:
        copy.wait()
    if last:
        mask_copy.wait()
    for source in range(layers):
        total = lax.dot_general(
            up_v[:, source * both :],
            dec_v[source, :, source * both :],
            (((1,), (1,)), ((), ())),
            preferred_element_type=jnp.float32,
        )
        if not first:
            acc_copies[source].wait()
            total = acc_v[source] + total
        if last:
            feat_v[source] = (total * feat_v[source].astype(jnp.float32)).astype(jnp.bfloat16)
        else:
            acc_v[source] = total
        out = pltpu.make_async_copy(
            (feat_v if last else acc_v).at[source], acc_out.at[source], out_sem.at[source]
        )
        out.start()
        outs.append(out)
    for out in outs:
        out.wait()


def run_round(meta, sparse, decoder, mask, acc, grad, mine, theirs, last):
    first = acc is None
    layers, width, rows = sparse.shape
    wide = mine[0].shape[2]
    pairs = decoder.shape[0]
    operands = [meta, sparse, decoder]
    if last:
        operands.append(mask)
    if not first:
        operands.append(acc)
    operands += mine + theirs
    aliases = {}
    if not first:
        aliases[len(operands)] = 0
        operands.append(grad)
    any_space = pl.BlockSpec(memory_space=pl.ANY)
    both = CORES * wide
    return pl.pallas_call(
        functools.partial(round_kernel, len(mine), layers, first, last),
        out_shape=(
            jax.ShapeDtypeStruct(decoder.shape, jnp.bfloat16),
            jax.ShapeDtypeStruct((layers, rows, width), jnp.bfloat16 if last else jnp.float32),
            jax.ShapeDtypeStruct((8, 128), jnp.float32),
        ),
        in_specs=[pl.BlockSpec(memory_space=pltpu.SMEM)] + [any_space] * (len(operands) - 1),
        out_specs=(any_space, any_space, pl.BlockSpec(memory_space=pltpu.VMEM)),
        scratch_shapes=[
            pltpu.VMEM((rows, layers * both), jnp.bfloat16),
            pltpu.VMEM((layers, width, rows), jnp.bfloat16),
            pltpu.VMEM((layers, width, layers * both), jnp.bfloat16),
            pltpu.VMEM((layers, rows, width), jnp.float32),
            pltpu.VMEM((pairs, width, both), jnp.bfloat16),
            pltpu.VMEM((layers, rows, width), jnp.bfloat16),
            pltpu.SemaphoreType.DMA((layers, CORES * len(mine))),
            pltpu.SemaphoreType.DMA((pairs,)),
            pltpu.SemaphoreType.DMA((2 + layers,)),
            pltpu.SemaphoreType.DMA((layers,)),
            pltpu.SemaphoreType.DMA((layers,)),
        ],
        input_output_aliases=aliases,
        cost_estimate=pl.CostEstimate(
            flops=2 * 4 * pairs * width * rows * both, bytes_accessed=20 * 2**20, transcendentals=0
        ),
        compiler_params=pltpu.CompilerParams(vmem_limit_bytes=VMEM_LIMIT),
    )(*operands)


def body(n_layer, n_feat, activations, active_blocks, cotangent, decoder):
    blocks = Gather(cotangent, n_layer, n_feat)
    planes = blocks.planes
    end = planes - 1
    sparse, mask = prepare(activations, active_blocks)
    core = lax.axis_index("feat") % CORES
    rows = [lax.axis_index("layer") ^ j for j in range(n_layer)]
    hops = range(1, planes)
    acc = grad = None
    for r in range(planes):
        blocks.sent = []
        if r == 0:
            blocks.straight(0)
            blocks.along_line(0, range(1, planes), hops)
            for near in range(1, min(3, planes)):
                blocks.straight(near)
            blocks.diagonal(0)
            for j in blocks.others:
                blocks.along_line(j, range(1, end), [1])
        else:
            if r + 2 < planes:
                blocks.straight(r + 2)
            for j in blocks.others:
                blocks.along_line(j, range(1, end), [r + 1])
        if r == max(end - 1, 0) and end > 0:
            blocks.diagonal(end)
        mine = [blocks.pieces[(r, j)] for j in range(n_layer)]
        theirs = [blocks.swap(blocks.tie(x)) for x in mine]
        plane = jnp.asarray([row[r] for row in blocks.order], jnp.int32)[blocks.plane]
        meta = jnp.stack([plane, core] + rows).astype(jnp.int32)
        meta = lax.optimization_barrier((meta, *blocks.sent))[0]
        grad, acc, blocks.token = run_round(
            meta, sparse, decoder, mask, acc, grad, mine, theirs, r == end
        )
    return grad, acc


def solution(mesh):
    in_specs = (
        P(None, None, ("layer", "feat")),
        P(None, None, ("layer", "feat")),
        P(None, "layer", "feat"),
        P(None, ("layer", "feat"), None),
    )
    out_specs = (P(None, ("layer", "feat"), None), P(None, None, ("layer", "feat")))
    work = functools.partial(body, mesh.shape["layer"], mesh.shape["feat"])
    return jax.shard_map(work, mesh=mesh, in_specs=in_specs, out_specs=out_specs, check_vma=False)
```

```python
import functools

import jax
import jax.numpy as jnp
from jax import lax
from jax.experimental import pallas as pl
from jax.experimental.pallas import tpu as pltpu
from jax.sharding import PartitionSpec as P

CORES = 2
VMEM_LIMIT = 60 * 2**20
CHUNK = 256


def plane_order(planes):
    return [
        sorted(range(planes), key=lambda p: (abs(p - z), p != (z ^ 1))) for z in range(planes)
    ]


def line_groups(order):
    groups = {}
    for z, row in enumerate(order):
        for r in range(1, len(row)):
            step = 1 if row[r] > z else -1
            held = order[z + step].index(row[r])
            groups.setdefault((abs(row[r] - z), r, held), []).append((z + step, z))
    return [(*key, groups[key]) for key in sorted(groups)]


class Gather:
    def __init__(self, block, sparse, n_layer, n_feat):
        self.sparse = self.ahead = sparse
        self.n_layer, self.n_feat = n_layer, n_feat
        self.planes = n_feat // CORES
        self.order = plane_order(self.planes)
        self.plane = lax.axis_index("feat") // CORES
        self.groups = line_groups(self.order)
        self.singles = [j for j in range(1, n_layer) if j & (j - 1) == 0]
        self.others = [j for j in range(1, n_layer) if j & (j - 1) != 0]
        self.pieces = {(0, 0): block}
        self.token = None
        self.tokens = []

    def tie(self, x):
        if self.token is None:
            return x
        x, token = lax.optimization_barrier((x, self.token))
        self.tokens.append(token)
        return x

    def permute(self, x, pairs):
        flat = [(l0 * self.n_feat + f0, l1 * self.n_feat + f1) for (l0, f0), (l1, f1) in pairs]
        return lax.ppermute(x, ("layer", "feat"), sorted(flat))

    def swap(self, x):
        every = [(l, f) for l in range(self.n_layer) for f in range(self.n_feat)]
        return self.permute(x, [((l, f), (l, f ^ 1)) for l, f in every])

    def across(self, r, j, bit):
        every = [(l, f) for l in range(self.n_layer) for f in range(self.n_feat)]
        x = self.tie(self.pieces[(r, j ^ bit)])
        self.pieces[(r, j)] = self.permute(x, [((l, f), (l ^ bit, f)) for l, f in every])

    def straight(self, r):
        for j in self.singles:
            self.across(r, j, j)

    def diagonal(self, r):
        for j in self.others:
            bits = [1 << b for b in range(j.bit_length()) if j >> b & 1]
            self.across(r, j, bits[0] if r == 0 else bits[-1])

    def along_line(self, j, rounds, hops):
        for dist, r, held, moves in self.groups:
            if r not in rounds or dist not in hops:
                continue
            pairs = [
                ((l, a * CORES + c), (l, b * CORES + c))
                for l in range(self.n_layer)
                for a, b in moves
                for c in range(CORES)
            ]
            x = self.tie(self.pieces[(held, j)])
            if dist > 1 and self.ahead is not None:
                x, self.sparse = lax.optimization_barrier((x, self.ahead))
                self.ahead = None
            got = self.permute(x, pairs)
            if (r, j) in self.pieces:
                here = functools.reduce(jnp.logical_or, [self.plane == b for _, b in moves])
                got = jnp.where(here, got, self.pieces[(r, j)])
            self.pieces[(r, j)] = got


def prepare_kernel(act, blocks, sparse, mask):
    width, rows = sparse.shape[1:]
    count = blocks.shape[1]
    bits = blocks[0].astype(jnp.float32)
    turned = jnp.concatenate(
        [jnp.broadcast_to(bits[b : b + 1], (width // count, rows)) for b in range(count)], axis=0
    ).astype(jnp.bfloat16)
    sparse[0] = act[0].T * turned
    mask[0] = turned.T


def prepare(activations, active_blocks):
    layers, rows, width = activations.shape
    count = active_blocks.shape[2]

    def block(*shape):
        return pl.BlockSpec((1, *shape), lambda s: (s, 0, 0))

    return pl.pallas_call(
        prepare_kernel,
        grid=(layers,),
        in_specs=[block(rows, width), block(count, rows)],
        out_specs=(block(width, rows), block(rows, width)),
        out_shape=(
            jax.ShapeDtypeStruct((layers, width, rows), jnp.bfloat16),
            jax.ShapeDtypeStruct((layers, rows, width), jnp.bfloat16),
        ),
        cost_estimate=pl.CostEstimate(flops=0, bytes_accessed=6 * layers * rows * width, transcendentals=0),
        compiler_params=pltpu.CompilerParams(vmem_limit_bytes=VMEM_LIMIT),
    )(activations, jnp.swapaxes(active_blocks, 1, 2))


def round_kernel(n_layer, n_tokens, layers, order, first, last, meta, sparse, decoder, *refs):
    refs = list(refs)
    mask = refs.pop(0) if last else None
    acc_in = None if first else refs.pop(0)
    parts = refs[: CORES * n_layer]
    refs = refs[CORES * n_layer :]
    if not first:
        refs.pop(0)
    refs = refs[n_tokens:]
    grad, acc_out, token = refs[:3]
    up_v, sparse_v, dec_v, acc_v, grad_v, feat_v, up_sem, dec_sem, in_sem, grad_sem, out_sem = refs[3:]
    tokens, wide = parts[0].shape[1:]
    both = CORES * wide
    width = decoder.shape[1]
    rows = n_layer * tokens
    plane = jnp.int32(order[0])
    for z in range(1, len(order)):
        plane = jnp.where(meta[0] == z, jnp.int32(order[z]), plane)
    columns = pl.ds(pl.multiple_of(plane * both, both), both)
    token[...] = jnp.zeros_like(token)

    copies = [pltpu.make_async_copy(sparse, sparse_v, in_sem.at[0])]
    ups = {}
    for target in range(layers):
        ups[target] = []
        for i, part in enumerate(parts):
            core = meta[1] if i < n_layer else 1 - meta[1]
            at_rows = pl.ds(pl.multiple_of((meta[2] ^ (i % n_layer)) * tokens, tokens), tokens)
            at_cols = pl.ds(pl.multiple_of(target * both + core * wide, wide), wide)
            ups[target].append(
                pltpu.make_async_copy(
                    part.at[target], up_v.at[at_rows, at_cols], up_sem.at[target, i]
                )
            )
    decs = []
    for target in range(layers):
        for source in range(target + 1):
            pair = target * (target + 1) // 2 + source
            decs.append(
                pltpu.make_async_copy(
                    decoder.at[pair, :, columns],
                    dec_v.at[source, :, pl.ds(target * both, both)],
                    dec_sem.at[pair],
                )
            )
    copies[0].start()
    for target in reversed(range(layers)):
        for copy in ups[target]:
            copy.start()
    for copy in decs:
        copy.start()
    acc_copies = []
    if not first:
        for source in range(layers):
            acc_copies.append(
                pltpu.make_async_copy(acc_in.at[source], acc_v.at[source], in_sem.at[2 + source])
            )
            acc_copies[-1].start()
    if last:
        mask_copy = pltpu.make_async_copy(mask, feat_v, in_sem.at[1])
        mask_copy.start()
    copies[0].wait()
    outs = []
    for target in reversed(range(layers)):
        for copy in ups[target]:
            copy.wait()
        count = target + 1
        base = target * (target + 1) // 2
        for source in range(count):
            for core in range(CORES):
                part = pl.ds(core * wide, wide)
                grad_v[base + source, :, part] = jnp.dot(
                    sparse_v[source],
                    up_v[:, target * both + core * wide : target * both + (core + 1) * wide],
                    preferred_element_type=jnp.float32,
                ).astype(jnp.bfloat16)
        out = pltpu.make_async_copy(
            grad_v.at[pl.ds(base, count)], grad.at[pl.ds(base, count), :, columns], grad_sem.at[target]
        )
        out.start()
        outs.append(out)
    for copy in decs:
        copy.wait()
    if last:
        mask_copy.wait()
    for source in range(layers):
        if not first:
            acc_copies[source].wait()
        for at in range(0, rows, CHUNK):
            total = lax.dot_general(
                up_v[at : at + CHUNK, source * both :],
                dec_v[source, :, source * both :],
                (((1,), (1,)), ((), ())),
                preferred_element_type=jnp.float32,
            )
            part = pl.ds(at, CHUNK)
            if not first:
                total = acc_v[source, part] + total
            if last:
                feat_v[source, part] = (total * feat_v[source, part].astype(jnp.float32)).astype(
                    jnp.bfloat16
                )
            else:
                acc_v[source, part] = total
        out = pltpu.make_async_copy(
            (feat_v if last else acc_v).at[source], acc_out.at[source], out_sem.at[source]
        )
        out.start()
        outs.append(out)
    for out in outs:
        out.wait()


def run_round(order, meta, tokens, sparse, decoder, mask, acc, grad, mine, theirs, last):
    first = acc is None
    layers, width, rows = sparse.shape
    wide = mine[0].shape[2]
    pairs = decoder.shape[0]
    operands = [meta, sparse, decoder]
    if last:
        operands.append(mask)
    if not first:
        operands.append(acc)
    operands += mine + theirs
    aliases = {}
    if not first:
        aliases[len(operands)] = 0
        operands.append(grad)
    operands += tokens
    any_space = pl.BlockSpec(memory_space=pl.ANY)
    both = CORES * wide
    return pl.pallas_call(
        functools.partial(round_kernel, len(mine), len(tokens), layers, order, first, last),
        out_shape=(
            jax.ShapeDtypeStruct(decoder.shape, jnp.bfloat16),
            jax.ShapeDtypeStruct((layers, rows, width), jnp.bfloat16 if last else jnp.float32),
            jax.ShapeDtypeStruct((8, 128), jnp.float32),
        ),
        in_specs=[pl.BlockSpec(memory_space=pltpu.SMEM)] + [any_space] * (len(operands) - 1),
        out_specs=(any_space, any_space, pl.BlockSpec(memory_space=pltpu.VMEM)),
        scratch_shapes=[
            pltpu.VMEM((rows, layers * both), jnp.bfloat16),
            pltpu.VMEM((layers, width, rows), jnp.bfloat16),
            pltpu.VMEM((layers, width, layers * both), jnp.bfloat16),
            pltpu.VMEM((layers, rows, width), jnp.float32),
            pltpu.VMEM((pairs, width, both), jnp.bfloat16),
            pltpu.VMEM((layers, rows, width), jnp.bfloat16),
            pltpu.SemaphoreType.DMA((layers, CORES * len(mine))),
            pltpu.SemaphoreType.DMA((pairs,)),
            pltpu.SemaphoreType.DMA((2 + layers,)),
            pltpu.SemaphoreType.DMA((layers,)),
            pltpu.SemaphoreType.DMA((layers,)),
        ],
        input_output_aliases=aliases,
        cost_estimate=pl.CostEstimate(
            flops=2 * 4 * pairs * width * rows * both, bytes_accessed=20 * 2**20, transcendentals=0
        ),
        compiler_params=pltpu.CompilerParams(vmem_limit_bytes=VMEM_LIMIT),
    )(*operands)


def body(n_layer, n_feat, activations, active_blocks, cotangent, decoder):
    sparse, mask = prepare(activations, active_blocks)
    blocks = Gather(cotangent, sparse, n_layer, n_feat)
    planes = blocks.planes
    end = planes - 1
    core = lax.axis_index("feat") % CORES
    place = jnp.stack([blocks.plane, core, lax.axis_index("layer")]).astype(jnp.int32)
    hops = range(1, planes)
    acc = grad = None
    for r in range(planes):
        if r == 0:
            blocks.straight(0)
            blocks.along_line(0, range(1, planes), hops)
            for near in range(1, min(3, planes)):
                blocks.straight(near)
            blocks.diagonal(0)
            for j in blocks.others:
                blocks.along_line(j, range(1, end), [1])
        else:
            if r + 2 < planes:
                blocks.straight(r + 2)
            for j in blocks.others:
                blocks.along_line(j, range(1, end), [r + 1])
        if r == max(end - 1, 0) and end > 0:
            blocks.diagonal(end)
        mine = [blocks.pieces[(r, j)] for j in range(n_layer)]
        theirs = [
            blocks.swap(blocks.tie(x) if j in blocks.others else x) for j, x in enumerate(mine)
        ]
        soon = [(r + 1, j) for j in blocks.singles] if r < end else []
        soon += [(r + 2, 0)] if r + 2 <= end else []
        place, *ready = lax.optimization_barrier((place, *[blocks.pieces[at] for at in soon]))
        blocks.pieces.update(zip(soon, ready))
        row = [row[r] for row in blocks.order]
        grad, acc, blocks.token = run_round(
            row, place, blocks.tokens, blocks.sparse, decoder, mask, acc, grad, mine, theirs, r == end
        )
        blocks.tokens = []
    return grad, acc


def solution(mesh):
    in_specs = (
        P(None, None, ("layer", "feat")),
        P(None, None, ("layer", "feat")),
        P(None, "layer", "feat"),
        P(None, ("layer", "feat"), None),
    )
    out_specs = (P(None, ("layer", "feat"), None), P(None, None, ("layer", "feat")))
    work = functools.partial(body, mesh.shape["layer"], mesh.shape["feat"])
    return jax.shard_map(work, mesh=mesh, in_specs=in_specs, out_specs=out_specs, check_vma=False)
```

```python
import functools

import jax
import jax.numpy as jnp
from jax import lax
from jax.experimental import pallas as pl
from jax.experimental.pallas import tpu as pltpu
from jax.sharding import PartitionSpec as P

CORES = 2
VMEM_LIMIT = 60 * 2**20
CHUNK = 256


def plane_order(planes):
    return [
        sorted(range(planes), key=lambda p: (abs(p - z), p != (z ^ 1))) for z in range(planes)
    ]


def line_groups(order):
    groups = {}
    for z, row in enumerate(order):
        for r in range(1, len(row)):
            step = 1 if row[r] > z else -1
            held = order[z + step].index(row[r])
            groups.setdefault((abs(row[r] - z), r, held), []).append((z + step, z))
    return [(*key, groups[key]) for key in sorted(groups)]


class Gather:
    def __init__(self, block, sparse, n_layer, n_feat):
        self.sparse = self.ahead = sparse
        self.n_layer, self.n_feat = n_layer, n_feat
        self.planes = n_feat // CORES
        self.order = plane_order(self.planes)
        self.plane = lax.axis_index("feat") // CORES
        self.groups = line_groups(self.order)
        self.singles = [j for j in range(1, n_layer) if j & (j - 1) == 0]
        self.others = [j for j in range(1, n_layer) if j & (j - 1) != 0]
        self.pieces = {(0, 0): block}
        self.later = {}
        self.token = None
        self.tokens = []

    def piece(self, r, j):
        if (r, j) in self.later:
            here, got = self.later.pop((r, j))
            self.pieces[(r, j)] = jnp.where(here, got, self.pieces[(r, j)])
        return self.pieces[(r, j)]

    def tie(self, x):
        if self.token is None:
            return x
        x, token = lax.optimization_barrier((x, self.token))
        self.tokens.append(token)
        return x

    def permute(self, x, pairs):
        flat = [(l0 * self.n_feat + f0, l1 * self.n_feat + f1) for (l0, f0), (l1, f1) in pairs]
        return lax.ppermute(x, ("layer", "feat"), sorted(flat))

    def swap(self, x):
        every = [(l, f) for l in range(self.n_layer) for f in range(self.n_feat)]
        return self.permute(x, [((l, f), (l, f ^ 1)) for l, f in every])

    def across(self, r, j, bit):
        every = [(l, f) for l in range(self.n_layer) for f in range(self.n_feat)]
        x = self.tie(self.piece(r, j ^ bit))
        self.pieces[(r, j)] = self.permute(x, [((l, f), (l ^ bit, f)) for l, f in every])

    def straight(self, r):
        for j in self.singles:
            self.across(r, j, j)

    def diagonal(self, r):
        for j in self.others:
            bits = [1 << b for b in range(j.bit_length()) if j >> b & 1]
            self.across(r, j, bits[0] if r == 0 else bits[-1])

    def along_line(self, j, rounds, hops):
        for dist, r, held, moves in self.groups:
            if r not in rounds or dist not in hops:
                continue
            pairs = [
                ((l, a * CORES + c), (l, b * CORES + c))
                for l in range(self.n_layer)
                for a, b in moves
                for c in range(CORES)
            ]
            x = self.tie(self.piece(held, j))
            if dist > 1 and self.ahead is not None:
                x, self.sparse = lax.optimization_barrier((x, self.ahead))
                self.ahead = None
            got = self.permute(x, pairs)
            if (r, j) in self.pieces:
                here = functools.reduce(jnp.logical_or, [self.plane == b for _, b in moves])
                self.later[(r, j)] = (here, got)
            else:
                self.pieces[(r, j)] = got


def prepare_kernel(act, blocks, sparse, mask):
    width, rows = sparse.shape[1:]
    count = blocks.shape[1]
    bits = blocks[0].astype(jnp.float32)
    turned = jnp.concatenate(
        [jnp.broadcast_to(bits[b : b + 1], (width // count, rows)) for b in range(count)], axis=0
    ).astype(jnp.bfloat16)
    sparse[0] = act[0].T * turned
    mask[0] = turned.T


def prepare(activations, active_blocks):
    layers, rows, width = activations.shape
    count = active_blocks.shape[2]

    def block(*shape):
        return pl.BlockSpec((1, *shape), lambda s: (s, 0, 0))

    return pl.pallas_call(
        prepare_kernel,
        grid=(layers,),
        in_specs=[block(rows, width), block(count, rows)],
        out_specs=(block(width, rows), block(rows, width)),
        out_shape=(
            jax.ShapeDtypeStruct((layers, width, rows), jnp.bfloat16),
            jax.ShapeDtypeStruct((layers, rows, width), jnp.bfloat16),
        ),
        cost_estimate=pl.CostEstimate(flops=0, bytes_accessed=6 * layers * rows * width, transcendentals=0),
        compiler_params=pltpu.CompilerParams(vmem_limit_bytes=VMEM_LIMIT),
    )(activations, jnp.swapaxes(active_blocks, 1, 2))


def round_kernel(n_layer, n_tokens, layers, order, first, last, meta, sparse, decoder, *refs):
    refs = list(refs)
    mask = refs.pop(0) if last else None
    acc_in = None if first else refs.pop(0)
    parts = refs[: CORES * n_layer]
    refs = refs[CORES * n_layer :]
    if not first:
        refs.pop(0)
    refs = refs[n_tokens:]
    grad, acc_out, token = refs[:3]
    up_v, sparse_v, dec_v, acc_v, grad_v, feat_v, up_sem, dec_sem, in_sem, grad_sem, out_sem = refs[3:]
    tokens, wide = parts[0].shape[1:]
    both = CORES * wide
    width = decoder.shape[1]
    rows = n_layer * tokens
    plane = jnp.int32(order[0])
    for z in range(1, len(order)):
        plane = jnp.where(meta[0] == z, jnp.int32(order[z]), plane)
    columns = pl.ds(pl.multiple_of(plane * both, both), both)
    token[...] = jnp.zeros_like(token)

    copies = [pltpu.make_async_copy(sparse, sparse_v, in_sem.at[0])]
    ups = {}
    for target in range(layers):
        ups[target] = []
        for i, part in enumerate(parts):
            core = meta[1] if i < n_layer else 1 - meta[1]
            at_rows = pl.ds(pl.multiple_of((meta[2] ^ (i % n_layer)) * tokens, tokens), tokens)
            at_cols = pl.ds(pl.multiple_of(target * both + core * wide, wide), wide)
            ups[target].append(
                pltpu.make_async_copy(
                    part.at[target], up_v.at[at_rows, at_cols], up_sem.at[target, i]
                )
            )
    decs = []
    for target in range(layers):
        for source in range(target + 1):
            pair = target * (target + 1) // 2 + source
            decs.append(
                pltpu.make_async_copy(
                    decoder.at[pair, :, columns],
                    dec_v.at[source, :, pl.ds(target * both, both)],
                    dec_sem.at[pair],
                )
            )
    copies[0].start()
    for target in reversed(range(layers)):
        for copy in ups[target]:
            copy.start()
    for copy in decs:
        copy.start()
    acc_copies = []
    if not first:
        for source in range(layers):
            acc_copies.append(
                pltpu.make_async_copy(acc_in.at[source], acc_v.at[source], in_sem.at[2 + source])
            )
            acc_copies[-1].start()
    if last:
        mask_copy = pltpu.make_async_copy(mask, feat_v, in_sem.at[1])
        mask_copy.start()
    copies[0].wait()
    outs = []
    for target in reversed(range(layers)):
        for copy in ups[target]:
            copy.wait()
        count = target + 1
        base = target * (target + 1) // 2
        for source in range(count):
            grad_v[base + source] = jnp.dot(
                sparse_v[source],
                up_v[:, target * both : (target + 1) * both],
                preferred_element_type=jnp.float32,
            ).astype(jnp.bfloat16)
        out = pltpu.make_async_copy(
            grad_v.at[pl.ds(base, count)], grad.at[pl.ds(base, count), :, columns], grad_sem.at[target]
        )
        out.start()
        outs.append(out)
    for copy in decs:
        copy.wait()
    if last:
        mask_copy.wait()
    def transposed_dot(a, b):
        return lax.dot_general(a, b, (((1,), (1,)), ((), ())), preferred_element_type=jnp.float32)

    for low in range(0, layers, 2):
        group = list(range(low, min(low + 2, layers)))
        high = group[-1]
        if not first:
            for source in group:
                acc_copies[source].wait()
        for at in range(0, rows, CHUNK):
            part = pl.ds(at, CHUNK)
            totals = transposed_dot(
                up_v[at : at + CHUNK, high * both :],
                dec_v[low : high + 1, :, high * both :].reshape(len(group) * width, -1),
            )
            for i, source in enumerate(group):
                total = totals[:, i * width : (i + 1) * width]
                if source < high:
                    own = slice(source * both, high * both)
                    total += transposed_dot(up_v[at : at + CHUNK, own], dec_v[source, :, own])
                if not first:
                    total += acc_v[source, part]
                if last:
                    total *= feat_v[source, part].astype(jnp.float32)
                    feat_v[source, part] = total.astype(jnp.bfloat16)
                else:
                    acc_v[source, part] = total
        for source in group:
            out = pltpu.make_async_copy(
                (feat_v if last else acc_v).at[source], acc_out.at[source], out_sem.at[source]
            )
            out.start()
            outs.append(out)
    for out in outs:
        out.wait()


def run_round(order, meta, tokens, sparse, decoder, mask, acc, grad, mine, theirs, last):
    first = acc is None
    layers, width, rows = sparse.shape
    wide = mine[0].shape[2]
    pairs = decoder.shape[0]
    operands = [meta, sparse, decoder]
    if last:
        operands.append(mask)
    if not first:
        operands.append(acc)
    operands += mine + theirs
    aliases = {}
    if not first:
        aliases[len(operands)] = 0
        operands.append(grad)
    operands += tokens
    any_space = pl.BlockSpec(memory_space=pl.ANY)
    both = CORES * wide
    return pl.pallas_call(
        functools.partial(round_kernel, len(mine), len(tokens), layers, order, first, last),
        out_shape=(
            jax.ShapeDtypeStruct(decoder.shape, jnp.bfloat16),
            jax.ShapeDtypeStruct((layers, rows, width), jnp.bfloat16 if last else jnp.float32),
            jax.ShapeDtypeStruct((8, 128), jnp.float32),
        ),
        in_specs=[pl.BlockSpec(memory_space=pltpu.SMEM)] + [any_space] * (len(operands) - 1),
        out_specs=(any_space, any_space, pl.BlockSpec(memory_space=pltpu.VMEM)),
        scratch_shapes=[
            pltpu.VMEM((rows, layers * both), jnp.bfloat16),
            pltpu.VMEM((layers, width, rows), jnp.bfloat16),
            pltpu.VMEM((layers, width, layers * both), jnp.bfloat16),
            pltpu.VMEM((layers, rows, width), jnp.float32),
            pltpu.VMEM((pairs, width, both), jnp.bfloat16),
            pltpu.VMEM((layers, rows, width), jnp.bfloat16),
            pltpu.SemaphoreType.DMA((layers, CORES * len(mine))),
            pltpu.SemaphoreType.DMA((pairs,)),
            pltpu.SemaphoreType.DMA((2 + layers,)),
            pltpu.SemaphoreType.DMA((layers,)),
            pltpu.SemaphoreType.DMA((layers,)),
        ],
        input_output_aliases=aliases,
        cost_estimate=pl.CostEstimate(
            flops=2 * 4 * pairs * width * rows * both, bytes_accessed=20 * 2**20, transcendentals=0
        ),
        compiler_params=pltpu.CompilerParams(vmem_limit_bytes=VMEM_LIMIT),
    )(*operands)


def body(n_layer, n_feat, activations, active_blocks, cotangent, decoder):
    sparse, mask = prepare(activations, active_blocks)
    blocks = Gather(cotangent, sparse, n_layer, n_feat)
    planes = blocks.planes
    end = planes - 1
    core = lax.axis_index("feat") % CORES
    place = jnp.stack([blocks.plane, core, lax.axis_index("layer")]).astype(jnp.int32)
    hops = range(1, planes)
    acc = grad = None
    for r in range(planes):
        if r == 0:
            blocks.straight(0)
            blocks.along_line(0, range(1, planes), hops)
            for near in range(1, min(3, planes)):
                blocks.straight(near)
            blocks.diagonal(0)
            for j in blocks.others:
                blocks.along_line(j, range(1, end), [1])
        else:
            if r + 2 < planes:
                blocks.straight(r + 2)
            for j in blocks.others:
                blocks.along_line(j, range(1, end), [r + 1])
        if r == max(end - 1, 0) and end > 0:
            blocks.diagonal(end)
        mine = [blocks.piece(r, j) for j in range(n_layer)]
        theirs = [
            blocks.swap(blocks.tie(x) if j in blocks.others else x) for j, x in enumerate(mine)
        ]
        soon = [(far, 0) for far in range(r + 1, planes) if far > r + 1 or r == 0]
        if r == 0 and end > 0:
            soon += [(1, j) for j in blocks.singles[1:]]
        if r == end - 1 and r > 0:
            soon += [(end, j) for j in blocks.singles[:1]]
        soon = [at for at in soon if at in blocks.pieces]
        place, *ready = lax.optimization_barrier((place, *[blocks.pieces[at] for at in soon]))
        blocks.pieces.update(zip(soon, ready))
        row = [row[r] for row in blocks.order]
        grad, acc, blocks.token = run_round(
            row, place, blocks.tokens, blocks.sparse, decoder, mask, acc, grad, mine, theirs, r == end
        )
        blocks.tokens = []
    return grad, acc


def solution(mesh):
    in_specs = (
        P(None, None, ("layer", "feat")),
        P(None, None, ("layer", "feat")),
        P(None, "layer", "feat"),
        P(None, ("layer", "feat"), None),
    )
    out_specs = (P(None, ("layer", "feat"), None), P(None, None, ("layer", "feat")))
    work = functools.partial(body, mesh.shape["layer"], mesh.shape["feat"])
    return jax.shard_map(work, mesh=mesh, in_specs=in_specs, out_specs=out_specs, check_vma=False)
```

```python
import functools

import jax
import jax.numpy as jnp
from jax import lax
from jax.experimental import pallas as pl
from jax.experimental.pallas import tpu as pltpu
from jax.sharding import PartitionSpec as P

CORES = 2
VMEM_LIMIT = 60 * 2**20
CHUNK = 256


def plane_order(planes):
    return [
        sorted(range(planes), key=lambda p: (abs(p - z), p != (z ^ 1))) for z in range(planes)
    ]


def line_groups(order):
    groups = {}
    for z, row in enumerate(order):
        for r in range(1, len(row)):
            step = 1 if row[r] > z else -1
            held = order[z + step].index(row[r])
            groups.setdefault((abs(row[r] - z), r, held), []).append((z + step, z))
    return [(*key, groups[key]) for key in sorted(groups)]


class Gather:
    def __init__(self, block, sparse, n_layer, n_feat):
        self.sparse = self.ahead = sparse
        self.n_layer, self.n_feat = n_layer, n_feat
        self.planes = n_feat // CORES
        self.order = plane_order(self.planes)
        self.plane = lax.axis_index("feat") // CORES
        self.groups = line_groups(self.order)
        self.singles = [j for j in range(1, n_layer) if j & (j - 1) == 0]
        self.others = [j for j in range(1, n_layer) if j & (j - 1) != 0]
        self.pieces = {(0, 0): block}
        self.later = {}
        self.token = None
        self.tokens = []

    def piece(self, r, j):
        if (r, j) in self.later:
            here, got = self.later.pop((r, j))
            self.pieces[(r, j)] = jnp.where(here, got, self.pieces[(r, j)])
        return self.pieces[(r, j)]

    def tie(self, x):
        if self.token is None:
            return x
        x, token = lax.optimization_barrier((x, self.token))
        self.tokens.append(token)
        return x

    def permute(self, x, pairs):
        flat = [(l0 * self.n_feat + f0, l1 * self.n_feat + f1) for (l0, f0), (l1, f1) in pairs]
        return lax.ppermute(x, ("layer", "feat"), sorted(flat))

    def swap(self, x):
        every = [(l, f) for l in range(self.n_layer) for f in range(self.n_feat)]
        return self.permute(x, [((l, f), (l, f ^ 1)) for l, f in every])

    def across(self, r, j, bit):
        every = [(l, f) for l in range(self.n_layer) for f in range(self.n_feat)]
        x = self.tie(self.piece(r, j ^ bit))
        self.pieces[(r, j)] = self.permute(x, [((l, f), (l ^ bit, f)) for l, f in every])

    def straight(self, r):
        for j in self.singles:
            self.across(r, j, j)

    def diagonal(self, r):
        for j in self.others:
            bits = [1 << b for b in range(j.bit_length()) if j >> b & 1]
            self.across(r, j, bits[0] if r == 0 else bits[-1])

    def along_line(self, j, rounds, hops):
        for dist, r, held, moves in self.groups:
            if r not in rounds or dist not in hops:
                continue
            pairs = [
                ((l, a * CORES + c), (l, b * CORES + c))
                for l in range(self.n_layer)
                for a, b in moves
                for c in range(CORES)
            ]
            x = self.tie(self.piece(held, j))
            if dist > 1 and self.ahead is not None:
                x, self.sparse = lax.optimization_barrier((x, self.ahead))
                self.ahead = None
            got = self.permute(x, pairs)
            if (r, j) in self.pieces:
                here = functools.reduce(jnp.logical_or, [self.plane == b for _, b in moves])
                self.later[(r, j)] = (here, got)
            else:
                self.pieces[(r, j)] = got


def prepare_kernel(act, blocks, sparse, mask):
    width, rows = sparse.shape[1:]
    count = blocks.shape[1]
    bits = blocks[0].astype(jnp.float32)
    turned = jnp.concatenate(
        [jnp.broadcast_to(bits[b : b + 1], (width // count, rows)) for b in range(count)], axis=0
    ).astype(jnp.bfloat16)
    sparse[0] = act[0].T * turned
    mask[0] = turned.T


def prepare(activations, active_blocks):
    layers, rows, width = activations.shape
    count = active_blocks.shape[2]

    def block(*shape):
        return pl.BlockSpec((1, *shape), lambda s: (s, 0, 0))

    return pl.pallas_call(
        prepare_kernel,
        grid=(layers,),
        in_specs=[block(rows, width), block(count, rows)],
        out_specs=(block(width, rows), block(rows, width)),
        out_shape=(
            jax.ShapeDtypeStruct((layers, width, rows), jnp.bfloat16),
            jax.ShapeDtypeStruct((layers, rows, width), jnp.bfloat16),
        ),
        cost_estimate=pl.CostEstimate(flops=0, bytes_accessed=6 * layers * rows * width, transcendentals=0),
        compiler_params=pltpu.CompilerParams(vmem_limit_bytes=VMEM_LIMIT),
    )(activations, jnp.swapaxes(active_blocks, 1, 2))


def round_kernel(n_layer, n_tokens, layers, order, first, last, meta, sparse, decoder, *refs):
    refs = list(refs)
    mask = refs.pop(0) if last else None
    acc_in = None if first else refs.pop(0)
    parts = refs[: CORES * n_layer]
    refs = refs[CORES * n_layer :]
    if not first:
        refs.pop(0)
    refs = refs[n_tokens:]
    grad, acc_out, token = refs[:3]
    up_v, sparse_v, dec_v, acc_v, grad_v, feat_v, up_sem, dec_sem, in_sem, grad_sem, out_sem = refs[3:]
    tokens, wide = parts[0].shape[1:]
    both = CORES * wide
    width = decoder.shape[1]
    rows = n_layer * tokens
    plane = jnp.int32(order[0])
    for z in range(1, len(order)):
        plane = jnp.where(meta[0] == z, jnp.int32(order[z]), plane)
    columns = pl.ds(pl.multiple_of(plane * both, both), both)
    token[...] = jnp.zeros_like(token)

    copies = [pltpu.make_async_copy(sparse, sparse_v, in_sem.at[0])]
    ups = {}
    for target in range(layers):
        ups[target] = []
        for i, part in enumerate(parts):
            core = meta[1] if i < n_layer else 1 - meta[1]
            at_rows = pl.ds(pl.multiple_of((meta[2] ^ (i % n_layer)) * tokens, tokens), tokens)
            at_cols = pl.ds(pl.multiple_of(target * both + core * wide, wide), wide)
            ups[target].append(
                pltpu.make_async_copy(
                    part.at[target], up_v.at[at_rows, at_cols], up_sem.at[target, i]
                )
            )
    decs = []
    for target in range(layers):
        for source in range(target + 1):
            pair = target * (target + 1) // 2 + source
            decs.append(
                pltpu.make_async_copy(
                    decoder.at[pair, :, columns],
                    dec_v.at[source, :, pl.ds(target * both, both)],
                    dec_sem.at[pair],
                )
            )
    copies[0].start()
    for target in reversed(range(layers)):
        for copy in ups[target]:
            copy.start()
    for copy in decs:
        copy.start()
    acc_copies = []
    if not first:
        for source in range(layers):
            acc_copies.append(
                pltpu.make_async_copy(acc_in.at[source], acc_v.at[source], in_sem.at[2 + source])
            )
            acc_copies[-1].start()
    if last:
        mask_copy = pltpu.make_async_copy(mask, feat_v, in_sem.at[1])
        mask_copy.start()
    copies[0].wait()
    for target in reversed(range(layers)):
        for copy in ups[target]:
            copy.wait()

    def grad_copy(pair):
        return pltpu.make_async_copy(grad_v.at[pair], grad.at[pair, :, columns], grad_sem.at[pair])

    @pl.loop(0, decoder.shape[0])
    def _(pair):
        target = sum((pair >= t * (t + 1) // 2).astype(jnp.int32) for t in range(1, layers))
        source = pair - target * (target + 1) // 2
        grad_v[pair] = jnp.dot(
            sparse_v[source],
            up_v[:, pl.ds(pl.multiple_of(target * both, both), both)],
            preferred_element_type=jnp.float32,
        ).astype(jnp.bfloat16)
        grad_copy(pair).start()

    for copy in decs:
        copy.wait()
    for copy in acc_copies:
        copy.wait()
    if last:
        mask_copy.wait()

    def transposed_dot(a, b):
        return lax.dot_general(a, b, (((1,), (1,)), ((), ())), preferred_element_type=jnp.float32)

    def acc_copy(at):
        part = pl.ds(pl.multiple_of(at * CHUNK, CHUNK), CHUNK)
        return pltpu.make_async_copy(
            (feat_v if last else acc_v).at[:, part], acc_out.at[:, part], out_sem.at[at]
        )

    @pl.loop(0, rows // CHUNK)
    def _(at):
        part = pl.ds(pl.multiple_of(at * CHUNK, CHUNK), CHUNK)
        for low in range(0, layers, 2):
            group = list(range(low, min(low + 2, layers)))
            high = group[-1]
            totals = transposed_dot(
                up_v[part, high * both :],
                dec_v[low : high + 1, :, high * both :].reshape(len(group) * width, -1),
            )
            for i, source in enumerate(group):
                total = totals[:, i * width : (i + 1) * width]
                if source < high:
                    own = slice(source * both, high * both)
                    total += transposed_dot(up_v[part, own], dec_v[source, :, own])
                if not first:
                    total += acc_v[source, part]
                if last:
                    total *= feat_v[source, part].astype(jnp.float32)
                    feat_v[source, part] = total.astype(jnp.bfloat16)
                else:
                    acc_v[source, part] = total
        acc_copy(at).start()

    for pair in range(decoder.shape[0]):
        grad_copy(pair).wait()
    for at in range(rows // CHUNK):
        acc_copy(at).wait()


def run_round(order, meta, tokens, sparse, decoder, mask, acc, grad, mine, theirs, last):
    first = acc is None
    layers, width, rows = sparse.shape
    wide = mine[0].shape[2]
    pairs = decoder.shape[0]
    operands = [meta, sparse, decoder]
    if last:
        operands.append(mask)
    if not first:
        operands.append(acc)
    operands += mine + theirs
    aliases = {}
    if not first:
        aliases[len(operands)] = 0
        operands.append(grad)
    operands += tokens
    any_space = pl.BlockSpec(memory_space=pl.ANY)
    both = CORES * wide
    return pl.pallas_call(
        functools.partial(round_kernel, len(mine), len(tokens), layers, order, first, last),
        out_shape=(
            jax.ShapeDtypeStruct(decoder.shape, jnp.bfloat16),
            jax.ShapeDtypeStruct((layers, rows, width), jnp.bfloat16 if last else jnp.float32),
            jax.ShapeDtypeStruct((8, 128), jnp.float32),
        ),
        in_specs=[pl.BlockSpec(memory_space=pltpu.SMEM)] + [any_space] * (len(operands) - 1),
        out_specs=(any_space, any_space, pl.BlockSpec(memory_space=pltpu.VMEM)),
        scratch_shapes=[
            pltpu.VMEM((rows, layers * both), jnp.bfloat16),
            pltpu.VMEM((layers, width, rows), jnp.bfloat16),
            pltpu.VMEM((layers, width, layers * both), jnp.bfloat16),
            pltpu.VMEM((layers, rows, width), jnp.float32),
            pltpu.VMEM((pairs, width, both), jnp.bfloat16),
            pltpu.VMEM((layers, rows, width), jnp.bfloat16),
            pltpu.SemaphoreType.DMA((layers, CORES * len(mine))),
            pltpu.SemaphoreType.DMA((pairs,)),
            pltpu.SemaphoreType.DMA((2 + layers,)),
            pltpu.SemaphoreType.DMA((pairs,)),
            pltpu.SemaphoreType.DMA((rows // CHUNK,)),
        ],
        input_output_aliases=aliases,
        cost_estimate=pl.CostEstimate(
            flops=2 * 4 * pairs * width * rows * both, bytes_accessed=20 * 2**20, transcendentals=0
        ),
        compiler_params=pltpu.CompilerParams(vmem_limit_bytes=VMEM_LIMIT),
    )(*operands)


def body(n_layer, n_feat, activations, active_blocks, cotangent, decoder):
    sparse, mask = prepare(activations, active_blocks)
    blocks = Gather(cotangent, sparse, n_layer, n_feat)
    planes = blocks.planes
    end = planes - 1
    core = lax.axis_index("feat") % CORES
    place = jnp.stack([blocks.plane, core, lax.axis_index("layer")]).astype(jnp.int32)
    hops = range(1, planes)
    acc = grad = None
    for r in range(planes):
        if r == 0:
            blocks.straight(0)
            blocks.along_line(0, range(1, planes), hops)
            for near in range(1, min(3, planes)):
                blocks.straight(near)
            blocks.diagonal(0)
            for j in blocks.others:
                blocks.along_line(j, range(1, end), [1])
        else:
            if r + 2 < planes:
                blocks.straight(r + 2)
            for j in blocks.others:
                blocks.along_line(j, range(1, end), [r + 1])
        if r == max(end - 1, 0) and end > 0:
            blocks.diagonal(end)
        mine = [blocks.piece(r, j) for j in range(n_layer)]
        theirs = [
            blocks.swap(blocks.tie(x) if j in blocks.others else x) for j, x in enumerate(mine)
        ]
        if r == 0:
            soon = [(far, 0) for far in range(1, planes)] + [(1, j) for j in blocks.singles[1:]]
        else:
            soon = [(r + 1, j) for j in blocks.singles]
        soon = [at for at in soon if at in blocks.pieces]
        place, *ready = lax.optimization_barrier((place, *[blocks.pieces[at] for at in soon]))
        blocks.pieces.update(zip(soon, ready))
        row = [row[r] for row in blocks.order]
        grad, acc, blocks.token = run_round(
            row, place, blocks.tokens, blocks.sparse, decoder, mask, acc, grad, mine, theirs, r == end
        )
        blocks.tokens = []
    return grad, acc


def solution(mesh):
    in_specs = (
        P(None, None, ("layer", "feat")),
        P(None, None, ("layer", "feat")),
        P(None, "layer", "feat"),
        P(None, ("layer", "feat"), None),
    )
    out_specs = (P(None, ("layer", "feat"), None), P(None, None, ("layer", "feat")))
    work = functools.partial(body, mesh.shape["layer"], mesh.shape["feat"])
    return jax.shard_map(work, mesh=mesh, in_specs=in_specs, out_specs=out_specs, check_vma=False)
```

```python
import functools

import jax
import jax.numpy as jnp
from jax import lax
from jax.experimental import pallas as pl
from jax.experimental.pallas import tpu as pltpu
from jax.sharding import PartitionSpec as P

CORES = 2
VMEM_LIMIT = 60 * 2**20
CHUNK = 256


def plane_order(planes):
    return [
        sorted(range(planes), key=lambda p: (abs(p - z), p != (z ^ 1))) for z in range(planes)
    ]


def line_groups(order):
    groups = {}
    for z, row in enumerate(order):
        for r in range(1, len(row)):
            step = 1 if row[r] > z else -1
            held = order[z + step].index(row[r])
            groups.setdefault((abs(row[r] - z), r, held), []).append((z + step, z))
    return [(*key, groups[key]) for key in sorted(groups)]


class Gather:
    def __init__(self, block, sparse, n_layer, n_feat):
        self.sparse = self.ahead = sparse
        self.n_layer, self.n_feat = n_layer, n_feat
        self.planes = n_feat // CORES
        self.order = plane_order(self.planes)
        self.plane = lax.axis_index("feat") // CORES
        self.groups = line_groups(self.order)
        self.singles = [j for j in range(1, n_layer) if j & (j - 1) == 0]
        self.others = [j for j in range(1, n_layer) if j & (j - 1) != 0]
        self.pieces = {(0, 0): block}
        self.later = {}
        self.token = None
        self.tokens = []

    def piece(self, r, j):
        if (r, j) in self.later:
            here, got = self.later.pop((r, j))
            self.pieces[(r, j)] = jnp.where(here, got, self.pieces[(r, j)])
        return self.pieces[(r, j)]

    def tie(self, x):
        if self.token is None:
            return x
        x, token = lax.optimization_barrier((x, self.token))
        self.tokens.append(token)
        return x

    def permute(self, x, pairs):
        flat = [(l0 * self.n_feat + f0, l1 * self.n_feat + f1) for (l0, f0), (l1, f1) in pairs]
        return lax.ppermute(x, ("layer", "feat"), sorted(flat))

    def swap(self, x):
        every = [(l, f) for l in range(self.n_layer) for f in range(self.n_feat)]
        return self.permute(x, [((l, f), (l, f ^ 1)) for l, f in every])

    def across(self, r, j, bit):
        every = [(l, f) for l in range(self.n_layer) for f in range(self.n_feat)]
        x = self.tie(self.piece(r, j ^ bit))
        self.pieces[(r, j)] = self.permute(x, [((l, f), (l ^ bit, f)) for l, f in every])

    def straight(self, r):
        for j in self.singles:
            self.across(r, j, j)

    def diagonal(self, r):
        for j in self.others:
            bits = [1 << b for b in range(j.bit_length()) if j >> b & 1]
            self.across(r, j, bits[0] if r == 0 else bits[-1])

    def along_line(self, j, rounds, hops):
        for dist, r, held, moves in self.groups:
            if r not in rounds or dist not in hops:
                continue
            pairs = [
                ((l, a * CORES + c), (l, b * CORES + c))
                for l in range(self.n_layer)
                for a, b in moves
                for c in range(CORES)
            ]
            x = self.tie(self.piece(held, j))
            if dist > 1 and self.ahead is not None:
                x, self.sparse = lax.optimization_barrier((x, self.ahead))
                self.ahead = None
            got = self.permute(x, pairs)
            if (r, j) in self.pieces:
                here = functools.reduce(jnp.logical_or, [self.plane == b for _, b in moves])
                self.later[(r, j)] = (here, got)
            else:
                self.pieces[(r, j)] = got


def prepare_kernel(act, blocks, sparse, mask):
    width, rows = sparse.shape[1:]
    count = blocks.shape[1]
    bits = blocks[0].astype(jnp.float32)
    turned = jnp.concatenate(
        [jnp.broadcast_to(bits[b : b + 1], (width // count, rows)) for b in range(count)], axis=0
    ).astype(jnp.bfloat16)
    sparse[0] = act[0].T * turned
    mask[0] = turned.T


def prepare(activations, active_blocks):
    layers, rows, width = activations.shape
    count = active_blocks.shape[2]

    def block(*shape):
        return pl.BlockSpec((1, *shape), lambda s: (s, 0, 0))

    return pl.pallas_call(
        prepare_kernel,
        grid=(layers,),
        in_specs=[block(rows, width), block(count, rows)],
        out_specs=(block(width, rows), block(rows, width)),
        out_shape=(
            jax.ShapeDtypeStruct((layers, width, rows), jnp.bfloat16),
            jax.ShapeDtypeStruct((layers, rows, width), jnp.bfloat16),
        ),
        cost_estimate=pl.CostEstimate(flops=0, bytes_accessed=6 * layers * rows * width, transcendentals=0),
        compiler_params=pltpu.CompilerParams(vmem_limit_bytes=VMEM_LIMIT),
    )(activations, jnp.swapaxes(active_blocks, 1, 2))


def round_kernel(n_layer, n_tokens, layers, order, first, last, meta, sparse, decoder, *refs):
    refs = list(refs)
    mask = refs.pop(0) if last else None
    acc_in = None if first else refs.pop(0)
    parts = refs[: CORES * n_layer]
    refs = refs[CORES * n_layer :]
    if not first:
        refs.pop(0)
    refs = refs[n_tokens:]
    grad, acc_out, token = refs[:3]
    up_v, sparse_v, dec_v, acc_v, grad_v, feat_v, up_sem, dec_sem, in_sem, grad_sem, out_sem = refs[3:]
    tokens, wide = parts[0].shape[1:]
    both = CORES * wide
    width = decoder.shape[1]
    rows = n_layer * tokens
    plane = jnp.int32(order[0])
    for z in range(1, len(order)):
        plane = jnp.where(meta[0] == z, jnp.int32(order[z]), plane)
    columns = pl.ds(pl.multiple_of(plane * both, both), both)
    token[...] = jnp.zeros_like(token)

    copies = [pltpu.make_async_copy(sparse, sparse_v, in_sem.at[0])]
    ups = {}
    for target in range(layers):
        ups[target] = []
        for i, part in enumerate(parts):
            core = meta[1] if i < n_layer else 1 - meta[1]
            at_rows = pl.ds(pl.multiple_of((meta[2] ^ (i % n_layer)) * tokens, tokens), tokens)
            at_cols = pl.ds(pl.multiple_of(target * both + core * wide, wide), wide)
            ups[target].append(
                pltpu.make_async_copy(
                    part.at[target], up_v.at[at_rows, at_cols], up_sem.at[target, i]
                )
            )
    decs = []
    for target in range(layers):
        for source in range(target + 1):
            pair = target * (target + 1) // 2 + source
            decs.append(
                pltpu.make_async_copy(
                    decoder.at[pair, :, columns],
                    dec_v.at[source, :, pl.ds(target * both, both)],
                    dec_sem.at[pair],
                )
            )
    copies[0].start()
    for target in reversed(range(layers)):
        for copy in ups[target]:
            copy.start()
    for copy in decs:
        copy.start()
    acc_copies = []
    if not first:
        for source in range(layers):
            acc_copies.append(
                pltpu.make_async_copy(acc_in.at[source], acc_v.at[source], in_sem.at[2 + source])
            )
            acc_copies[-1].start()
    if last:
        mask_copy = pltpu.make_async_copy(mask, feat_v, in_sem.at[1])
        mask_copy.start()
    copies[0].wait()
    outs = []
    for target in reversed(range(layers)):
        for copy in ups[target]:
            copy.wait()
        count = target + 1
        base = target * (target + 1) // 2
        for source in range(count):
            grad_v[base + source] = jnp.dot(
                sparse_v[source],
                up_v[:, target * both : (target + 1) * both],
                preferred_element_type=jnp.float32,
            ).astype(jnp.bfloat16)
        out = pltpu.make_async_copy(
            grad_v.at[pl.ds(base, count)], grad.at[pl.ds(base, count), :, columns], grad_sem.at[target]
        )
        out.start()
        outs.append(out)
    for copy in decs:
        copy.wait()
    if last:
        mask_copy.wait()
    def transposed_dot(a, b):
        return lax.dot_general(a, b, (((1,), (1,)), ((), ())), preferred_element_type=jnp.float32)

    for low in range(0, layers, 2):
        group = list(range(low, min(low + 2, layers)))
        high = group[-1]
        if not first:
            for source in group:
                acc_copies[source].wait()
        for at in range(0, rows, CHUNK):
            part = pl.ds(at, CHUNK)
            totals = transposed_dot(
                up_v[at : at + CHUNK, high * both :],
                dec_v[low : high + 1, :, high * both :].reshape(len(group) * width, -1),
            )
            for i, source in enumerate(group):
                total = totals[:, i * width : (i + 1) * width]
                if source < high:
                    own = slice(source * both, high * both)
                    total += transposed_dot(up_v[at : at + CHUNK, own], dec_v[source, :, own])
                if not first:
                    total += acc_v[source, part]
                if last:
                    total *= feat_v[source, part].astype(jnp.float32)
                    feat_v[source, part] = total.astype(jnp.bfloat16)
                else:
                    acc_v[source, part] = total
        for source in group:
            out = pltpu.make_async_copy(
                (feat_v if last else acc_v).at[source], acc_out.at[source], out_sem.at[source]
            )
            out.start()
            outs.append(out)
    for out in outs:
        out.wait()


def run_round(order, meta, tokens, sparse, decoder, mask, acc, grad, mine, theirs, last):
    first = acc is None
    layers, width, rows = sparse.shape
    wide = mine[0].shape[2]
    pairs = decoder.shape[0]
    operands = [meta, sparse, decoder]
    if last:
        operands.append(mask)
    if not first:
        operands.append(acc)
    operands += mine + theirs
    aliases = {}
    if not first:
        aliases[len(operands)] = 0
        operands.append(grad)
    operands += tokens
    any_space = pl.BlockSpec(memory_space=pl.ANY)
    both = CORES * wide
    return pl.pallas_call(
        functools.partial(round_kernel, len(mine), len(tokens), layers, order, first, last),
        out_shape=(
            jax.ShapeDtypeStruct(decoder.shape, jnp.bfloat16),
            jax.ShapeDtypeStruct((layers, rows, width), jnp.bfloat16 if last else jnp.float32),
            jax.ShapeDtypeStruct((8, 128), jnp.float32),
        ),
        in_specs=[pl.BlockSpec(memory_space=pltpu.SMEM)] + [any_space] * (len(operands) - 1),
        out_specs=(any_space, any_space, pl.BlockSpec(memory_space=pltpu.VMEM)),
        scratch_shapes=[
            pltpu.VMEM((rows, layers * both), jnp.bfloat16),
            pltpu.VMEM((layers, width, rows), jnp.bfloat16),
            pltpu.VMEM((layers, width, layers * both), jnp.bfloat16),
            pltpu.VMEM((layers, rows, width), jnp.float32),
            pltpu.VMEM((pairs, width, both), jnp.bfloat16),
            pltpu.VMEM((layers, rows, width), jnp.bfloat16),
            pltpu.SemaphoreType.DMA((layers, CORES * len(mine))),
            pltpu.SemaphoreType.DMA((pairs,)),
            pltpu.SemaphoreType.DMA((2 + layers,)),
            pltpu.SemaphoreType.DMA((layers,)),
            pltpu.SemaphoreType.DMA((layers,)),
        ],
        input_output_aliases=aliases,
        cost_estimate=pl.CostEstimate(
            flops=2 * 4 * pairs * width * rows * both, bytes_accessed=20 * 2**20, transcendentals=0
        ),
        compiler_params=pltpu.CompilerParams(vmem_limit_bytes=VMEM_LIMIT),
    )(*operands)


def body(n_layer, n_feat, activations, active_blocks, cotangent, decoder):
    sparse, mask = prepare(activations, active_blocks)
    blocks = Gather(cotangent, sparse, n_layer, n_feat)
    planes = blocks.planes
    end = planes - 1
    core = lax.axis_index("feat") % CORES
    place = jnp.stack([blocks.plane, core, lax.axis_index("layer")]).astype(jnp.int32)
    hops = range(1, planes)
    acc = grad = None
    for r in range(planes):
        if r == 0:
            blocks.straight(0)
            blocks.along_line(0, range(1, planes), hops)
            for near in range(1, min(3, planes)):
                blocks.straight(near)
            blocks.diagonal(0)
            for j in blocks.others:
                blocks.along_line(j, range(1, end), [1])
        else:
            if r + 2 < planes:
                blocks.straight(r + 2)
            for j in blocks.others:
                blocks.along_line(j, range(1, end), [r + 1])
        if r == max(end - 1, 0) and end > 0:
            blocks.diagonal(end)
        mine = [blocks.piece(r, j) for j in range(n_layer)]
        theirs = [
            blocks.swap(blocks.tie(x) if r > 1 or j in blocks.others else x)
            for j, x in enumerate(mine)
        ]
        if r == 0:
            soon = [(far, 0) for far in range(1, planes)] + [(1, j) for j in blocks.singles[1:]]
        else:
            soon = [(r + 1, j) for j in blocks.singles[: None if r == end - 1 else 1]]
        soon = [at for at in soon if at in blocks.pieces]
        place, *ready = lax.optimization_barrier((place, *[blocks.pieces[at] for at in soon]))
        blocks.pieces.update(zip(soon, ready))
        row = [row[r] for row in blocks.order]
        grad, acc, blocks.token = run_round(
            row, place, blocks.tokens, blocks.sparse, decoder, mask, acc, grad, mine, theirs, r == end
        )
        blocks.tokens = []
    return grad, acc


def solution(mesh):
    in_specs = (
        P(None, None, ("layer", "feat")),
        P(None, None, ("layer", "feat")),
        P(None, "layer", "feat"),
        P(None, ("layer", "feat"), None),
    )
    out_specs = (P(None, ("layer", "feat"), None), P(None, None, ("layer", "feat")))
    work = functools.partial(body, mesh.shape["layer"], mesh.shape["feat"])
    return jax.shard_map(work, mesh=mesh, in_specs=in_specs, out_specs=out_specs, check_vma=False)
```

```python
import functools

import jax
import jax.numpy as jnp
from jax import lax
from jax.experimental import pallas as pl
from jax.experimental.pallas import tpu as pltpu
from jax.sharding import PartitionSpec as P

CORES = 2
VMEM_LIMIT = 60 * 2**20
CHUNK = 256


def plane_order(planes):
    return [
        sorted(range(planes), key=lambda p: (abs(p - z), p != (z ^ 1))) for z in range(planes)
    ]


def line_groups(order):
    groups = {}
    for z, row in enumerate(order):
        for r in range(1, len(row)):
            step = 1 if row[r] > z else -1
            held = order[z + step].index(row[r])
            groups.setdefault((abs(row[r] - z), r, held), []).append((z + step, z))
    return [(*key, groups[key]) for key in sorted(groups)]


class Gather:
    def __init__(self, block, sparse, n_layer, n_feat):
        self.sparse = self.ahead = sparse
        self.n_layer, self.n_feat = n_layer, n_feat
        self.planes = n_feat // CORES
        self.order = plane_order(self.planes)
        self.plane = lax.axis_index("feat") // CORES
        self.groups = line_groups(self.order)
        self.singles = [j for j in range(1, n_layer) if j & (j - 1) == 0]
        self.others = [j for j in range(1, n_layer) if j & (j - 1) != 0]
        self.pieces = {(0, 0): block}
        self.later = {}
        self.token = None
        self.tokens = []

    def piece(self, r, j):
        if (r, j) in self.later:
            here, got = self.later.pop((r, j))
            self.pieces[(r, j)] = jnp.where(here, got, self.pieces[(r, j)])
        return self.pieces[(r, j)]

    def tie(self, x):
        if self.token is None:
            return x
        x, token = lax.optimization_barrier((x, self.token))
        self.tokens.append(token)
        return x

    def permute(self, x, pairs):
        flat = [(l0 * self.n_feat + f0, l1 * self.n_feat + f1) for (l0, f0), (l1, f1) in pairs]
        return lax.ppermute(x, ("layer", "feat"), sorted(flat))

    def swap(self, x):
        every = [(l, f) for l in range(self.n_layer) for f in range(self.n_feat)]
        return self.permute(x, [((l, f), (l, f ^ 1)) for l, f in every])

    def across(self, r, j, bit):
        every = [(l, f) for l in range(self.n_layer) for f in range(self.n_feat)]
        x = self.tie(self.piece(r, j ^ bit))
        self.pieces[(r, j)] = self.permute(x, [((l, f), (l ^ bit, f)) for l, f in every])

    def straight(self, r):
        for j in self.singles:
            self.across(r, j, j)

    def diagonal(self, r):
        for j in self.others:
            bits = [1 << b for b in range(j.bit_length()) if j >> b & 1]
            self.across(r, j, bits[0] if r < 2 else bits[-1])

    def along_line(self, j, rounds, hops):
        for dist, r, held, moves in self.groups:
            if r not in rounds or dist not in hops:
                continue
            pairs = [
                ((l, a * CORES + c), (l, b * CORES + c))
                for l in range(self.n_layer)
                for a, b in moves
                for c in range(CORES)
            ]
            x = self.tie(self.piece(held, j))
            if dist > 1 and self.ahead is not None:
                x, self.sparse = lax.optimization_barrier((x, self.ahead))
                self.ahead = None
            got = self.permute(x, pairs)
            if (r, j) in self.pieces:
                here = functools.reduce(jnp.logical_or, [self.plane == b for _, b in moves])
                self.later[(r, j)] = (here, got)
            else:
                self.pieces[(r, j)] = got


def prepare_kernel(act, blocks, sparse, mask):
    width, rows = sparse.shape[1:]
    count = blocks.shape[1]
    bits = blocks[0].astype(jnp.float32)
    turned = jnp.concatenate(
        [jnp.broadcast_to(bits[b : b + 1], (width // count, rows)) for b in range(count)], axis=0
    ).astype(jnp.bfloat16)
    sparse[0] = act[0].T * turned
    mask[0] = turned.T


def prepare(activations, active_blocks):
    layers, rows, width = activations.shape
    count = active_blocks.shape[2]

    def block(*shape):
        return pl.BlockSpec((1, *shape), lambda s: (s, 0, 0))

    return pl.pallas_call(
        prepare_kernel,
        grid=(layers,),
        in_specs=[block(rows, width), block(count, rows)],
        out_specs=(block(width, rows), block(rows, width)),
        out_shape=(
            jax.ShapeDtypeStruct((layers, width, rows), jnp.bfloat16),
            jax.ShapeDtypeStruct((layers, rows, width), jnp.bfloat16),
        ),
        cost_estimate=pl.CostEstimate(flops=0, bytes_accessed=6 * layers * rows * width, transcendentals=0),
        compiler_params=pltpu.CompilerParams(vmem_limit_bytes=VMEM_LIMIT),
    )(activations, jnp.swapaxes(active_blocks, 1, 2))


def round_kernel(n_layer, n_tokens, layers, order, first, last, meta, sparse, decoder, *refs):
    refs = list(refs)
    mask = refs.pop(0) if last else None
    acc_in = None if first else refs.pop(0)
    parts = refs[: CORES * n_layer]
    refs = refs[CORES * n_layer :]
    if not first:
        refs.pop(0)
    refs = refs[n_tokens:]
    grad, acc_out, token = refs[:3]
    up_v, sparse_v, dec_v, acc_v, grad_v, feat_v, up_sem, dec_sem, in_sem, grad_sem, out_sem = refs[3:]
    tokens, wide = parts[0].shape[1:]
    both = CORES * wide
    width = decoder.shape[1]
    rows = n_layer * tokens
    plane = jnp.int32(order[0])
    for z in range(1, len(order)):
        plane = jnp.where(meta[0] == z, jnp.int32(order[z]), plane)
    columns = pl.ds(pl.multiple_of(plane * both, both), both)
    token[...] = jnp.zeros_like(token)

    copies = [pltpu.make_async_copy(sparse, sparse_v, in_sem.at[0])]
    ups = {}
    for target in range(layers):
        ups[target] = []
        for i, part in enumerate(parts):
            core = meta[1] if i < n_layer else 1 - meta[1]
            at_rows = pl.ds(pl.multiple_of((meta[2] ^ (i % n_layer)) * tokens, tokens), tokens)
            at_cols = pl.ds(pl.multiple_of(target * both + core * wide, wide), wide)
            ups[target].append(
                pltpu.make_async_copy(
                    part.at[target], up_v.at[at_rows, at_cols], up_sem.at[target, i]
                )
            )
    decs = []
    for target in range(layers):
        for source in range(target + 1):
            pair = target * (target + 1) // 2 + source
            decs.append(
                pltpu.make_async_copy(
                    decoder.at[pair, :, columns],
                    dec_v.at[source, :, pl.ds(target * both, both)],
                    dec_sem.at[pair],
                )
            )
    copies[0].start()
    for target in reversed(range(layers)):
        for copy in ups[target]:
            copy.start()
    for copy in decs:
        copy.start()
    acc_copies = []
    if not first:
        for source in range(layers):
            acc_copies.append(
                pltpu.make_async_copy(acc_in.at[source], acc_v.at[source], in_sem.at[2 + source])
            )
            acc_copies[-1].start()
    if last:
        mask_copy = pltpu.make_async_copy(mask, feat_v, in_sem.at[1])
        mask_copy.start()
    copies[0].wait()
    outs = []
    for target in reversed(range(layers)):
        for copy in ups[target]:
            copy.wait()
        count = target + 1
        base = target * (target + 1) // 2
        for source in range(count):
            grad_v[base + source] = jnp.dot(
                sparse_v[source],
                up_v[:, target * both : (target + 1) * both],
                preferred_element_type=jnp.float32,
            ).astype(jnp.bfloat16)
        out = pltpu.make_async_copy(
            grad_v.at[pl.ds(base, count)], grad.at[pl.ds(base, count), :, columns], grad_sem.at[target]
        )
        out.start()
        outs.append(out)
    for copy in decs:
        copy.wait()
    if last:
        mask_copy.wait()
    def transposed_dot(a, b):
        return lax.dot_general(a, b, (((1,), (1,)), ((), ())), preferred_element_type=jnp.float32)

    for low in range(0, layers, 2):
        group = list(range(low, min(low + 2, layers)))
        high = group[-1]
        if not first:
            for source in group:
                acc_copies[source].wait()
        for at in range(0, rows, CHUNK):
            part = pl.ds(at, CHUNK)
            totals = transposed_dot(
                up_v[at : at + CHUNK, high * both :],
                dec_v[low : high + 1, :, high * both :].reshape(len(group) * width, -1),
            )
            for i, source in enumerate(group):
                total = totals[:, i * width : (i + 1) * width]
                if source < high:
                    own = slice(source * both, high * both)
                    total += transposed_dot(up_v[at : at + CHUNK, own], dec_v[source, :, own])
                if not first:
                    total += acc_v[source, part]
                if last:
                    total *= feat_v[source, part].astype(jnp.float32)
                    feat_v[source, part] = total.astype(jnp.bfloat16)
                else:
                    acc_v[source, part] = total
        for source in group:
            out = pltpu.make_async_copy(
                (feat_v if last else acc_v).at[source], acc_out.at[source], out_sem.at[source]
            )
            out.start()
            outs.append(out)
    for out in outs:
        out.wait()


def run_round(order, meta, tokens, sparse, decoder, mask, acc, grad, mine, theirs, last):
    first = acc is None
    layers, width, rows = sparse.shape
    wide = mine[0].shape[2]
    pairs = decoder.shape[0]
    operands = [meta, sparse, decoder]
    if last:
        operands.append(mask)
    if not first:
        operands.append(acc)
    operands += mine + theirs
    aliases = {}
    if not first:
        aliases[len(operands)] = 0
        operands.append(grad)
    operands += tokens
    any_space = pl.BlockSpec(memory_space=pl.ANY)
    both = CORES * wide
    return pl.pallas_call(
        functools.partial(round_kernel, len(mine), len(tokens), layers, order, first, last),
        out_shape=(
            jax.ShapeDtypeStruct(decoder.shape, jnp.bfloat16),
            jax.ShapeDtypeStruct((layers, rows, width), jnp.bfloat16 if last else jnp.float32),
            jax.ShapeDtypeStruct((8, 128), jnp.float32),
        ),
        in_specs=[pl.BlockSpec(memory_space=pltpu.SMEM)] + [any_space] * (len(operands) - 1),
        out_specs=(any_space, any_space, pl.BlockSpec(memory_space=pltpu.VMEM)),
        scratch_shapes=[
            pltpu.VMEM((rows, layers * both), jnp.bfloat16),
            pltpu.VMEM((layers, width, rows), jnp.bfloat16),
            pltpu.VMEM((layers, width, layers * both), jnp.bfloat16),
            pltpu.VMEM((layers, rows, width), jnp.float32),
            pltpu.VMEM((pairs, width, both), jnp.bfloat16),
            pltpu.VMEM((layers, rows, width), jnp.bfloat16),
            pltpu.SemaphoreType.DMA((layers, CORES * len(mine))),
            pltpu.SemaphoreType.DMA((pairs,)),
            pltpu.SemaphoreType.DMA((2 + layers,)),
            pltpu.SemaphoreType.DMA((layers,)),
            pltpu.SemaphoreType.DMA((layers,)),
        ],
        input_output_aliases=aliases,
        cost_estimate=pl.CostEstimate(
            flops=2 * 4 * pairs * width * rows * both, bytes_accessed=20 * 2**20, transcendentals=0
        ),
        compiler_params=pltpu.CompilerParams(vmem_limit_bytes=VMEM_LIMIT),
    )(*operands)


def body(n_layer, n_feat, activations, active_blocks, cotangent, decoder):
    sparse, mask = prepare(activations, active_blocks)
    blocks = Gather(cotangent, sparse, n_layer, n_feat)
    planes = blocks.planes
    end = planes - 1
    core = lax.axis_index("feat") % CORES
    place = jnp.stack([blocks.plane, core, lax.axis_index("layer")]).astype(jnp.int32)
    hops = range(1, planes)
    acc = grad = None
    for r in range(planes):
        if r == 0:
            blocks.straight(0)
            blocks.along_line(0, range(1, planes), hops)
            for near in range(1, min(3, planes)):
                blocks.straight(near)
            blocks.diagonal(0)
            if end > 1:
                blocks.diagonal(1)
            for j in blocks.others:
                blocks.along_line(j, range(2, end), [1])
        else:
            if r + 2 < planes:
                blocks.straight(r + 2)
            for j in blocks.others:
                blocks.along_line(j, range(2, end), [r + 1])
        if r == max(end - 1, 0) and end > 0:
            blocks.diagonal(end)
        mine = [blocks.piece(r, j) for j in range(n_layer)]
        theirs = [
            blocks.swap(blocks.tie(x) if r > 1 or j in blocks.others else x)
            for j, x in enumerate(mine)
        ]
        if r == 0:
            soon = [(far, 0) for far in range(1, planes)] + [(1, j) for j in blocks.singles[1:]]
        else:
            soon = [(r + 1, j) for j in blocks.singles[0 if r == end - 1 else 1 :]]
        soon = [at for at in soon if at in blocks.pieces]
        place, *ready = lax.optimization_barrier((place, *[blocks.pieces[at] for at in soon]))
        blocks.pieces.update(zip(soon, ready))
        row = [row[r] for row in blocks.order]
        grad, acc, blocks.token = run_round(
            row, place, blocks.tokens, blocks.sparse, decoder, mask, acc, grad, mine, theirs, r == end
        )
        blocks.tokens = []
    return grad, acc


def solution(mesh):
    in_specs = (
        P(None, None, ("layer", "feat")),
        P(None, None, ("layer", "feat")),
        P(None, "layer", "feat"),
        P(None, ("layer", "feat"), None),
    )
    out_specs = (P(None, ("layer", "feat"), None), P(None, None, ("layer", "feat")))
    work = functools.partial(body, mesh.shape["layer"], mesh.shape["feat"])
    return jax.shard_map(work, mesh=mesh, in_specs=in_specs, out_specs=out_specs, check_vma=False)
```

```python
import functools

import jax
import jax.numpy as jnp
from jax import lax
from jax.experimental import pallas as pl
from jax.experimental.pallas import tpu as pltpu
from jax.sharding import PartitionSpec as P

CORES = 2
VMEM_LIMIT = 60 * 2**20
CHUNK = 256


def plane_order(planes):
    return [
        sorted(range(planes), key=lambda p: (abs(p - z), p != (z ^ 1))) for z in range(planes)
    ]


def line_groups(order):
    groups = {}
    for z, row in enumerate(order):
        for r in range(1, len(row)):
            step = 1 if row[r] > z else -1
            held = order[z + step].index(row[r])
            groups.setdefault((abs(row[r] - z), r, held), []).append((z + step, z))
    return [(*key, groups[key]) for key in sorted(groups)]


class Gather:
    def __init__(self, block, sparse, n_layer, n_feat):
        self.sparse = self.ahead = sparse
        self.n_layer, self.n_feat = n_layer, n_feat
        self.planes = n_feat // CORES
        self.order = plane_order(self.planes)
        self.plane = lax.axis_index("feat") // CORES
        self.groups = line_groups(self.order)
        self.singles = [j for j in range(1, n_layer) if j & (j - 1) == 0]
        self.others = [j for j in range(1, n_layer) if j & (j - 1) != 0]
        self.pieces = {(0, 0): block}
        self.later = {}
        self.token = None
        self.tokens = []

    def piece(self, r, j):
        if (r, j) in self.later:
            here, got = self.later.pop((r, j))
            self.pieces[(r, j)] = jnp.where(here, got, self.pieces[(r, j)])
        return self.pieces[(r, j)]

    def tie(self, x):
        if self.token is None:
            return x
        x, token = lax.optimization_barrier((x, self.token))
        self.tokens.append(token)
        return x

    def permute(self, x, pairs):
        flat = [(l0 * self.n_feat + f0, l1 * self.n_feat + f1) for (l0, f0), (l1, f1) in pairs]
        return lax.ppermute(x, ("layer", "feat"), sorted(flat))

    def swap(self, x):
        every = [(l, f) for l in range(self.n_layer) for f in range(self.n_feat)]
        return self.permute(x, [((l, f), (l, f ^ 1)) for l, f in every])

    def across(self, r, j, bit):
        every = [(l, f) for l in range(self.n_layer) for f in range(self.n_feat)]
        x = self.tie(self.piece(r, j ^ bit))
        self.pieces[(r, j)] = self.permute(x, [((l, f), (l ^ bit, f)) for l, f in every])

    def straight(self, r):
        for j in self.singles:
            self.across(r, j, j)

    def diagonal(self, r):
        for j in self.others:
            bits = [1 << b for b in range(j.bit_length()) if j >> b & 1]
            self.across(r, j, bits[0] if r < 2 else bits[-1])

    def along_line(self, j, rounds, hops):
        for dist, r, held, moves in self.groups:
            if r not in rounds or dist not in hops:
                continue
            pairs = [
                ((l, a * CORES + c), (l, b * CORES + c))
                for l in range(self.n_layer)
                for a, b in moves
                for c in range(CORES)
            ]
            x = self.tie(self.piece(held, j))
            if dist > 1 and self.ahead is not None:
                x, self.sparse = lax.optimization_barrier((x, self.ahead))
                self.ahead = None
            got = self.permute(x, pairs)
            if (r, j) in self.pieces:
                here = functools.reduce(jnp.logical_or, [self.plane == b for _, b in moves])
                self.later[(r, j)] = (here, got)
            else:
                self.pieces[(r, j)] = got


def prepare_kernel(act, blocks, sparse, mask):
    width, rows = sparse.shape[1:]
    count = blocks.shape[1]
    bits = blocks[0].astype(jnp.float32)
    turned = jnp.concatenate(
        [jnp.broadcast_to(bits[b : b + 1], (width // count, rows)) for b in range(count)], axis=0
    ).astype(jnp.bfloat16)
    sparse[0] = act[0].T * turned
    mask[0] = turned.T


def prepare(activations, active_blocks):
    layers, rows, width = activations.shape
    count = active_blocks.shape[2]

    def block(*shape):
        return pl.BlockSpec((1, *shape), lambda s: (s, 0, 0))

    return pl.pallas_call(
        prepare_kernel,
        grid=(layers,),
        in_specs=[block(rows, width), block(count, rows)],
        out_specs=(block(width, rows), block(rows, width)),
        out_shape=(
            jax.ShapeDtypeStruct((layers, width, rows), jnp.bfloat16),
            jax.ShapeDtypeStruct((layers, rows, width), jnp.bfloat16),
        ),
        cost_estimate=pl.CostEstimate(flops=0, bytes_accessed=6 * layers * rows * width, transcendentals=0),
        compiler_params=pltpu.CompilerParams(vmem_limit_bytes=VMEM_LIMIT),
    )(activations, jnp.swapaxes(active_blocks, 1, 2))


def round_kernel(n_layer, n_tokens, layers, order, first, last, meta, sparse, decoder, *refs):
    refs = list(refs)
    mask = refs.pop(0) if last else None
    acc_in = None if first else refs.pop(0)
    parts = refs[: CORES * n_layer]
    refs = refs[CORES * n_layer :]
    if not first:
        refs.pop(0)
    refs = refs[n_tokens:]
    grad, acc_out, token = refs[:3]
    up_v, sparse_v, dec_v, acc_v, grad_v, feat_v, up_sem, dec_sem, in_sem, grad_sem, out_sem = refs[3:]
    tokens, wide = parts[0].shape[1:]
    both = CORES * wide
    width = decoder.shape[1]
    rows = n_layer * tokens
    plane = jnp.int32(order[0])
    for z in range(1, len(order)):
        plane = jnp.where(meta[0] == z, jnp.int32(order[z]), plane)
    columns = pl.ds(pl.multiple_of(plane * both, both), both)
    token[...] = jnp.zeros_like(token)

    copies = [pltpu.make_async_copy(sparse, sparse_v, in_sem.at[0])]
    ups = {}
    for target in range(layers):
        ups[target] = []
        for i, part in enumerate(parts):
            core = meta[1] if i < n_layer else 1 - meta[1]
            at_rows = pl.ds(pl.multiple_of((meta[2] ^ (i % n_layer)) * tokens, tokens), tokens)
            at_cols = pl.ds(pl.multiple_of(target * both + core * wide, wide), wide)
            ups[target].append(
                pltpu.make_async_copy(
                    part.at[target], up_v.at[at_rows, at_cols], up_sem.at[target, i]
                )
            )
    decs = []
    for target in range(layers):
        for source in range(target + 1):
            pair = target * (target + 1) // 2 + source
            decs.append(
                pltpu.make_async_copy(
                    decoder.at[pair, :, columns],
                    dec_v.at[source, :, pl.ds(target * both, both)],
                    dec_sem.at[pair],
                )
            )
    copies[0].start()
    for target in reversed(range(layers)):
        for copy in ups[target]:
            copy.start()
    for copy in decs:
        copy.start()
    acc_copies = []
    if not first:
        for source in range(layers):
            acc_copies.append(
                pltpu.make_async_copy(acc_in.at[source], acc_v.at[source], in_sem.at[2 + source])
            )
            acc_copies[-1].start()
    if last:
        mask_copy = pltpu.make_async_copy(mask, feat_v, in_sem.at[1])
        mask_copy.start()
    copies[0].wait()
    outs = []
    for target in reversed(range(layers)):
        for copy in ups[target]:
            copy.wait()
        count = target + 1
        base = target * (target + 1) // 2
        for source in range(count):
            grad_v[base + source] = jnp.dot(
                sparse_v[source],
                up_v[:, target * both : (target + 1) * both],
                preferred_element_type=jnp.float32,
            ).astype(jnp.bfloat16)
        out = pltpu.make_async_copy(
            grad_v.at[pl.ds(base, count)], grad.at[pl.ds(base, count), :, columns], grad_sem.at[target]
        )
        out.start()
        outs.append(out)
    for copy in decs:
        copy.wait()
    if last:
        mask_copy.wait()
    def transposed_dot(a, b):
        return lax.dot_general(a, b, (((1,), (1,)), ((), ())), preferred_element_type=jnp.float32)

    for low in range(0, layers, 2):
        group = list(range(low, min(low + 2, layers)))
        high = group[-1]
        if not first:
            for source in group:
                acc_copies[source].wait()
        for at in range(0, rows, CHUNK):
            part = pl.ds(at, CHUNK)
            totals = transposed_dot(
                up_v[at : at + CHUNK, high * both :],
                dec_v[low : high + 1, :, high * both :].reshape(len(group) * width, -1),
            )
            for i, source in enumerate(group):
                total = totals[:, i * width : (i + 1) * width]
                if source < high:
                    own = slice(source * both, high * both)
                    total += transposed_dot(up_v[at : at + CHUNK, own], dec_v[source, :, own])
                if not first:
                    total += acc_v[source, part]
                if last:
                    total *= feat_v[source, part].astype(jnp.float32)
                    feat_v[source, part] = total.astype(jnp.bfloat16)
                else:
                    acc_v[source, part] = total
        for source in group:
            out = pltpu.make_async_copy(
                (feat_v if last else acc_v).at[source], acc_out.at[source], out_sem.at[source]
            )
            out.start()
            outs.append(out)
    for out in outs:
        out.wait()


def run_round(order, meta, tokens, sparse, decoder, mask, acc, grad, mine, theirs, last):
    first = acc is None
    layers, width, rows = sparse.shape
    wide = mine[0].shape[2]
    pairs = decoder.shape[0]
    operands = [meta, sparse, decoder]
    if last:
        operands.append(mask)
    if not first:
        operands.append(acc)
    operands += mine + theirs
    aliases = {}
    if not first:
        aliases[len(operands)] = 0
        operands.append(grad)
    operands += tokens
    any_space = pl.BlockSpec(memory_space=pl.ANY)
    both = CORES * wide
    return pl.pallas_call(
        functools.partial(round_kernel, len(mine), len(tokens), layers, order, first, last),
        out_shape=(
            jax.ShapeDtypeStruct(decoder.shape, jnp.bfloat16),
            jax.ShapeDtypeStruct((layers, rows, width), jnp.bfloat16 if last else jnp.float32),
            jax.ShapeDtypeStruct((8, 128), jnp.float32),
        ),
        in_specs=[pl.BlockSpec(memory_space=pltpu.SMEM)] + [any_space] * (len(operands) - 1),
        out_specs=(any_space, any_space, pl.BlockSpec(memory_space=pltpu.VMEM)),
        scratch_shapes=[
            pltpu.VMEM((rows, layers * both), jnp.bfloat16),
            pltpu.VMEM((layers, width, rows), jnp.bfloat16),
            pltpu.VMEM((layers, width, layers * both), jnp.bfloat16),
            pltpu.VMEM((layers, rows, width), jnp.float32),
            pltpu.VMEM((pairs, width, both), jnp.bfloat16),
            pltpu.VMEM((layers, rows, width), jnp.bfloat16),
            pltpu.SemaphoreType.DMA((layers, CORES * len(mine))),
            pltpu.SemaphoreType.DMA((pairs,)),
            pltpu.SemaphoreType.DMA((2 + layers,)),
            pltpu.SemaphoreType.DMA((layers,)),
            pltpu.SemaphoreType.DMA((layers,)),
        ],
        input_output_aliases=aliases,
        cost_estimate=pl.CostEstimate(
            flops=2 * 4 * pairs * width * rows * both, bytes_accessed=20 * 2**20, transcendentals=0
        ),
        compiler_params=pltpu.CompilerParams(vmem_limit_bytes=VMEM_LIMIT),
    )(*operands)


def body(n_layer, n_feat, activations, active_blocks, cotangent, decoder):
    sparse, mask = prepare(activations, active_blocks)
    blocks = Gather(cotangent, sparse, n_layer, n_feat)
    planes = blocks.planes
    end = planes - 1
    core = lax.axis_index("feat") % CORES
    place = jnp.stack([blocks.plane, core, lax.axis_index("layer")]).astype(jnp.int32)
    hops = range(1, planes)
    acc = grad = None
    for r in range(planes):
        if r == 0:
            blocks.straight(0)
            blocks.along_line(0, range(1, planes), hops)
            for near in range(1, min(3, planes)):
                blocks.straight(near)
            blocks.diagonal(0)
            if end > 1:
                blocks.diagonal(1)
            for j in blocks.others:
                blocks.along_line(j, range(2, end), [1])
        else:
            if r + 2 < planes:
                blocks.straight(r + 2)
            for j in blocks.others:
                blocks.along_line(j, range(2, end), [r + 1])
        if r == max(end - 1, 0) and end > 0:
            blocks.diagonal(end)
        mine = [blocks.piece(r, j) for j in range(n_layer)]
        if r == 1 and end > 2:
            held = [(1, j) for j in blocks.others] + [(end, 0)]
            ready = lax.optimization_barrier([blocks.piece(*at) for at in held])
            blocks.pieces.update(zip(held, ready))
            mine = [blocks.piece(r, j) for j in range(n_layer)]
        free = [0] + blocks.singles if r in (0, 1, end) else []
        theirs = [blocks.swap(x if j in free else blocks.tie(x)) for j, x in enumerate(mine)]
        if r == 0:
            soon = [(far, 0) for far in range(1, planes)] + [(1, j) for j in blocks.singles[1:]]
        else:
            soon = [(r + 1, j) for j in blocks.singles[0 if r == end - 1 else 1 :]]
        soon = [at for at in soon if at in blocks.pieces]
        place, *ready = lax.optimization_barrier((place, *[blocks.pieces[at] for at in soon]))
        blocks.pieces.update(zip(soon, ready))
        row = [row[r] for row in blocks.order]
        grad, acc, blocks.token = run_round(
            row, place, blocks.tokens, blocks.sparse, decoder, mask, acc, grad, mine, theirs, r == end
        )
        blocks.tokens = []
    return grad, acc


def solution(mesh):
    in_specs = (
        P(None, None, ("layer", "feat")),
        P(None, None, ("layer", "feat")),
        P(None, "layer", "feat"),
        P(None, ("layer", "feat"), None),
    )
    out_specs = (P(None, ("layer", "feat"), None), P(None, None, ("layer", "feat")))
    work = functools.partial(body, mesh.shape["layer"], mesh.shape["feat"])
    return jax.shard_map(work, mesh=mesh, in_specs=in_specs, out_specs=out_specs, check_vma=False)
```

```python
import functools

import jax
import jax.numpy as jnp
from jax import lax
from jax.experimental import pallas as pl
from jax.experimental.pallas import tpu as pltpu
from jax.sharding import PartitionSpec as P

CORES = 2
VMEM_LIMIT = 60 * 2**20
CHUNK = 256


def plane_order(planes):
    return [
        sorted(range(planes), key=lambda p: (abs(p - z), p != (z ^ 1))) for z in range(planes)
    ]


def line_groups(order):
    groups = {}
    for z, row in enumerate(order):
        for r in range(1, len(row)):
            step = 1 if row[r] > z else -1
            held = order[z + step].index(row[r])
            groups.setdefault((abs(row[r] - z), r, held), []).append((z + step, z))
    return [(*key, groups[key]) for key in sorted(groups)]


class Gather:
    def __init__(self, block, sparse, n_layer, n_feat):
        self.sparse = self.ahead = sparse
        self.n_layer, self.n_feat = n_layer, n_feat
        self.planes = n_feat // CORES
        self.order = plane_order(self.planes)
        self.plane = lax.axis_index("feat") // CORES
        self.groups = line_groups(self.order)
        self.singles = [j for j in range(1, n_layer) if j & (j - 1) == 0]
        self.others = [j for j in range(1, n_layer) if j & (j - 1) != 0]
        self.pieces = {(0, 0): block}
        self.later = {}
        self.token = None
        self.tokens = []

    def piece(self, r, j):
        if (r, j) in self.later:
            here, got = self.later.pop((r, j))
            self.pieces[(r, j)] = jnp.where(here, got, self.pieces[(r, j)])
        return self.pieces[(r, j)]

    def tie(self, x):
        if self.token is None:
            return x
        x, token = lax.optimization_barrier((x, self.token))
        self.tokens.append(token)
        return x

    def permute(self, x, pairs):
        flat = [(l0 * self.n_feat + f0, l1 * self.n_feat + f1) for (l0, f0), (l1, f1) in pairs]
        return lax.ppermute(x, ("layer", "feat"), sorted(flat))

    def swap(self, x):
        every = [(l, f) for l in range(self.n_layer) for f in range(self.n_feat)]
        return self.permute(x, [((l, f), (l, f ^ 1)) for l, f in every])

    def across(self, r, j, bit):
        every = [(l, f) for l in range(self.n_layer) for f in range(self.n_feat)]
        x = self.tie(self.piece(r, j ^ bit))
        self.pieces[(r, j)] = self.permute(x, [((l, f), (l ^ bit, f)) for l, f in every])

    def straight(self, r):
        for j in self.singles:
            self.across(r, j, j)

    def diagonal(self, r):
        for j in self.others:
            bits = [1 << b for b in range(j.bit_length()) if j >> b & 1]
            self.across(r, j, bits[0] if r < 2 else bits[-1])

    def along_line(self, j, rounds, hops):
        for dist, r, held, moves in self.groups:
            if r not in rounds or dist not in hops:
                continue
            pairs = [
                ((l, a * CORES + c), (l, b * CORES + c))
                for l in range(self.n_layer)
                for a, b in moves
                for c in range(CORES)
            ]
            x = self.tie(self.piece(held, j))
            if dist > 1 and self.ahead is not None:
                x, self.sparse = lax.optimization_barrier((x, self.ahead))
                self.ahead = None
            got = self.permute(x, pairs)
            if (r, j) in self.pieces:
                here = functools.reduce(jnp.logical_or, [self.plane == b for _, b in moves])
                self.later[(r, j)] = (here, got)
            else:
                self.pieces[(r, j)] = got


def prepare_kernel(act, blocks, sparse, mask):
    width, rows = sparse.shape[1:]
    count = blocks.shape[1]
    bits = blocks[0].astype(jnp.float32)
    turned = jnp.concatenate(
        [jnp.broadcast_to(bits[b : b + 1], (width // count, rows)) for b in range(count)], axis=0
    ).astype(jnp.bfloat16)
    sparse[0] = act[0].T * turned
    mask[0] = turned.T


def prepare(activations, active_blocks):
    layers, rows, width = activations.shape
    count = active_blocks.shape[2]

    def block(*shape):
        return pl.BlockSpec((1, *shape), lambda s: (s, 0, 0))

    return pl.pallas_call(
        prepare_kernel,
        grid=(layers,),
        in_specs=[block(rows, width), block(count, rows)],
        out_specs=(block(width, rows), block(rows, width)),
        out_shape=(
            jax.ShapeDtypeStruct((layers, width, rows), jnp.bfloat16),
            jax.ShapeDtypeStruct((layers, rows, width), jnp.bfloat16),
        ),
        cost_estimate=pl.CostEstimate(flops=0, bytes_accessed=6 * layers * rows * width, transcendentals=0),
        compiler_params=pltpu.CompilerParams(vmem_limit_bytes=VMEM_LIMIT),
    )(activations, jnp.swapaxes(active_blocks, 1, 2))


def round_kernel(n_layer, n_tokens, layers, order, first, last, meta, sparse, decoder, *refs):
    refs = list(refs)
    mask = refs.pop(0) if last else None
    acc_in = None if first else refs.pop(0)
    parts = refs[: CORES * n_layer]
    refs = refs[CORES * n_layer :]
    if not first:
        refs.pop(0)
    refs = refs[n_tokens:]
    grad, acc_out, token = refs[:3]
    up_v, sparse_v, dec_v, acc_v, grad_v, feat_v, *sems = refs[3:]
    up_sem, sparse_sem, dec_sem, in_sem, grad_sem, out_sem = sems
    tokens, wide = parts[0].shape[1:]
    both = CORES * wide
    width = decoder.shape[1]
    rows = n_layer * tokens
    plane = jnp.int32(order[0])
    for z in range(1, len(order)):
        plane = jnp.where(meta[0] == z, jnp.int32(order[z]), plane)
    columns = pl.ds(pl.multiple_of(plane * both, both), both)
    token[...] = jnp.zeros_like(token)

    sparse_copies = [
        pltpu.make_async_copy(sparse.at[source], sparse_v.at[source], sparse_sem.at[source])
        for source in range(layers)
    ]
    ups = {}
    for target in range(layers):
        ups[target] = []
        for i, part in enumerate(parts):
            core = meta[1] if i < n_layer else 1 - meta[1]
            at_rows = pl.ds(pl.multiple_of((meta[2] ^ (i % n_layer)) * tokens, tokens), tokens)
            at_cols = pl.ds(pl.multiple_of(target * both + core * wide, wide), wide)
            ups[target].append(
                pltpu.make_async_copy(
                    part.at[target], up_v.at[at_rows, at_cols], up_sem.at[target, i]
                )
            )
    decs = []
    for target in range(layers):
        for source in range(target + 1):
            pair = target * (target + 1) // 2 + source
            decs.append(
                pltpu.make_async_copy(
                    decoder.at[pair, :, columns],
                    dec_v.at[source, :, pl.ds(target * both, both)],
                    dec_sem.at[pair],
                )
            )
    early = layers - 2 if layers > 1 else 0
    sparse_copies[0].start()
    for copy in ups[layers - 1]:
        copy.start()
    for copy in sparse_copies[1:]:
        copy.start()
    for target in reversed(range(early, layers - 1)):
        for copy in ups[target]:
            copy.start()
    for copy in ups[layers - 1]:
        copy.wait()
    for target in reversed(range(early)):
        for copy in ups[target]:
            copy.start()
    for copy in decs:
        copy.start()
    acc_copies = []
    if not first:
        for source in range(layers):
            acc_copies.append(
                pltpu.make_async_copy(acc_in.at[source], acc_v.at[source], in_sem.at[1 + source])
            )
            acc_copies[-1].start()
    if last:
        mask_copy = pltpu.make_async_copy(mask, feat_v, in_sem.at[0])
        mask_copy.start()
    outs = []
    for target in reversed(range(layers)):
        if target < layers - 1:
            for copy in ups[target]:
                copy.wait()
        count = target + 1
        base = target * (target + 1) // 2
        for source in range(count):
            if target == layers - 1:
                sparse_copies[source].wait()
            grad_v[base + source] = jnp.dot(
                sparse_v[source],
                up_v[:, target * both : (target + 1) * both],
                preferred_element_type=jnp.float32,
            ).astype(jnp.bfloat16)
        out = pltpu.make_async_copy(
            grad_v.at[pl.ds(base, count)], grad.at[pl.ds(base, count), :, columns], grad_sem.at[target]
        )
        out.start()
        outs.append(out)
    for copy in decs:
        copy.wait()
    if last:
        mask_copy.wait()
    def transposed_dot(a, b):
        return lax.dot_general(a, b, (((1,), (1,)), ((), ())), preferred_element_type=jnp.float32)

    for low in range(0, layers, 2):
        group = list(range(low, min(low + 2, layers)))
        high = group[-1]
        if not first:
            for source in group:
                acc_copies[source].wait()
        for at in range(0, rows, CHUNK):
            part = pl.ds(at, CHUNK)
            totals = transposed_dot(
                up_v[at : at + CHUNK, high * both :],
                dec_v[low : high + 1, :, high * both :].reshape(len(group) * width, -1),
            )
            for i, source in enumerate(group):
                total = totals[:, i * width : (i + 1) * width]
                if source < high:
                    own = slice(source * both, high * both)
                    total += transposed_dot(up_v[at : at + CHUNK, own], dec_v[source, :, own])
                if not first:
                    total += acc_v[source, part]
                if last:
                    total *= feat_v[source, part].astype(jnp.float32)
                    feat_v[source, part] = total.astype(jnp.bfloat16)
                else:
                    acc_v[source, part] = total
        for source in group:
            out = pltpu.make_async_copy(
                (feat_v if last else acc_v).at[source], acc_out.at[source], out_sem.at[source]
            )
            out.start()
            outs.append(out)
    for out in outs:
        out.wait()


def run_round(order, meta, tokens, sparse, decoder, mask, acc, grad, mine, theirs, last):
    first = acc is None
    layers, width, rows = sparse.shape
    wide = mine[0].shape[2]
    pairs = decoder.shape[0]
    operands = [meta, sparse, decoder]
    if last:
        operands.append(mask)
    if not first:
        operands.append(acc)
    operands += mine + theirs
    aliases = {}
    if not first:
        aliases[len(operands)] = 0
        operands.append(grad)
    operands += tokens
    any_space = pl.BlockSpec(memory_space=pl.ANY)
    both = CORES * wide
    return pl.pallas_call(
        functools.partial(round_kernel, len(mine), len(tokens), layers, order, first, last),
        out_shape=(
            jax.ShapeDtypeStruct(decoder.shape, jnp.bfloat16),
            jax.ShapeDtypeStruct((layers, rows, width), jnp.bfloat16 if last else jnp.float32),
            jax.ShapeDtypeStruct((8, 128), jnp.float32),
        ),
        in_specs=[pl.BlockSpec(memory_space=pltpu.SMEM)] + [any_space] * (len(operands) - 1),
        out_specs=(any_space, any_space, pl.BlockSpec(memory_space=pltpu.VMEM)),
        scratch_shapes=[
            pltpu.VMEM((rows, layers * both), jnp.bfloat16),
            pltpu.VMEM((layers, width, rows), jnp.bfloat16),
            pltpu.VMEM((layers, width, layers * both), jnp.bfloat16),
            pltpu.VMEM((layers, rows, width), jnp.float32),
            pltpu.VMEM((pairs, width, both), jnp.bfloat16),
            pltpu.VMEM((layers, rows, width), jnp.bfloat16),
            pltpu.SemaphoreType.DMA((layers, CORES * len(mine))),
            pltpu.SemaphoreType.DMA((layers,)),
            pltpu.SemaphoreType.DMA((pairs,)),
            pltpu.SemaphoreType.DMA((1 + layers,)),
            pltpu.SemaphoreType.DMA((layers,)),
            pltpu.SemaphoreType.DMA((layers,)),
        ],
        input_output_aliases=aliases,
        cost_estimate=pl.CostEstimate(
            flops=2 * 4 * pairs * width * rows * both, bytes_accessed=20 * 2**20, transcendentals=0
        ),
        compiler_params=pltpu.CompilerParams(vmem_limit_bytes=VMEM_LIMIT),
    )(*operands)


def body(n_layer, n_feat, activations, active_blocks, cotangent, decoder):
    sparse, mask = prepare(activations, active_blocks)
    blocks = Gather(cotangent, sparse, n_layer, n_feat)
    planes = blocks.planes
    end = planes - 1
    core = lax.axis_index("feat") % CORES
    place = jnp.stack([blocks.plane, core, lax.axis_index("layer")]).astype(jnp.int32)
    hops = range(1, planes)
    acc = grad = None
    for r in range(planes):
        if r == 0:
            blocks.straight(0)
            blocks.along_line(0, range(1, planes), hops)
            for near in range(1, min(3, planes)):
                blocks.straight(near)
            blocks.diagonal(0)
            if end > 1:
                blocks.diagonal(1)
            for j in blocks.others:
                blocks.along_line(j, range(2, end), [1])
        else:
            if r + 2 < planes:
                blocks.straight(r + 2)
            for j in blocks.others:
                blocks.along_line(j, range(2, end), [r + 1])
        if r == max(end - 1, 0) and end > 0:
            blocks.diagonal(end)
        mine = [blocks.piece(r, j) for j in range(n_layer)]
        if r == 1 and end > 2:
            held = [(1, j) for j in blocks.others] + [(end, 0)]
            ready = lax.optimization_barrier([blocks.piece(*at) for at in held])
            blocks.pieces.update(zip(held, ready))
            mine = [blocks.piece(r, j) for j in range(n_layer)]
        free = [0] + blocks.singles if r in (0, 1, end) else []
        theirs = [blocks.swap(x if j in free else blocks.tie(x)) for j, x in enumerate(mine)]
        if r == 0:
            soon = [(far, 0) for far in range(1, planes)] + [(1, j) for j in blocks.singles[1:]]
        else:
            soon = [(r + 1, j) for j in blocks.singles[0 if r == end - 1 else 1 :]]
        soon = [at for at in soon if at in blocks.pieces]
        place, *ready = lax.optimization_barrier((place, *[blocks.pieces[at] for at in soon]))
        blocks.pieces.update(zip(soon, ready))
        row = [row[r] for row in blocks.order]
        grad, acc, blocks.token = run_round(
            row, place, blocks.tokens, blocks.sparse, decoder, mask, acc, grad, mine, theirs, r == end
        )
        blocks.tokens = []
    return grad, acc


def solution(mesh):
    in_specs = (
        P(None, None, ("layer", "feat")),
        P(None, None, ("layer", "feat")),
        P(None, "layer", "feat"),
        P(None, ("layer", "feat"), None),
    )
    out_specs = (P(None, ("layer", "feat"), None), P(None, None, ("layer", "feat")))
    work = functools.partial(body, mesh.shape["layer"], mesh.shape["feat"])
    return jax.shard_map(work, mesh=mesh, in_specs=in_specs, out_specs=out_specs, check_vma=False)
```

```python
import functools

import jax
import jax.numpy as jnp
from jax import lax
from jax.experimental import pallas as pl
from jax.experimental.pallas import tpu as pltpu
from jax.sharding import PartitionSpec as P

CORES = 2
VMEM_LIMIT = 60 * 2**20
CHUNK = 256


def plane_order(planes):
    return [
        sorted(range(planes), key=lambda p: (abs(p - z), p != (z ^ 1))) for z in range(planes)
    ]


def line_groups(order):
    groups = {}
    for z, row in enumerate(order):
        for r in range(1, len(row)):
            step = 1 if row[r] > z else -1
            held = order[z + step].index(row[r])
            groups.setdefault((abs(row[r] - z), r, held), []).append((z + step, z))
    return [(*key, groups[key]) for key in sorted(groups)]


class Gather:
    def __init__(self, block, sparse, n_layer, n_feat):
        self.sparse = self.ahead = sparse
        self.n_layer, self.n_feat = n_layer, n_feat
        self.planes = n_feat // CORES
        self.order = plane_order(self.planes)
        self.plane = lax.axis_index("feat") // CORES
        self.groups = line_groups(self.order)
        self.singles = [j for j in range(1, n_layer) if j & (j - 1) == 0]
        self.others = [j for j in range(1, n_layer) if j & (j - 1) != 0]
        self.pieces = {(0, 0): block}
        self.later = {}
        self.token = None
        self.tokens = []

    def piece(self, r, j):
        if (r, j) in self.later:
            here, got = self.later.pop((r, j))
            self.pieces[(r, j)] = jnp.where(here, got, self.pieces[(r, j)])
        return self.pieces[(r, j)]

    def tie(self, x):
        if self.token is None:
            return x
        x, token = lax.optimization_barrier((x, self.token))
        self.tokens.append(token)
        return x

    def permute(self, x, pairs):
        flat = [(l0 * self.n_feat + f0, l1 * self.n_feat + f1) for (l0, f0), (l1, f1) in pairs]
        return lax.ppermute(x, ("layer", "feat"), sorted(flat))

    def swap(self, x):
        every = [(l, f) for l in range(self.n_layer) for f in range(self.n_feat)]
        return self.permute(x, [((l, f), (l, f ^ 1)) for l, f in every])

    def across(self, r, j, bit):
        every = [(l, f) for l in range(self.n_layer) for f in range(self.n_feat)]
        x = self.tie(self.piece(r, j ^ bit))
        self.pieces[(r, j)] = self.permute(x, [((l, f), (l ^ bit, f)) for l, f in every])

    def straight(self, r):
        for j in self.singles:
            self.across(r, j, j)

    def diagonal(self, r):
        for j in self.others:
            bits = [1 << b for b in range(j.bit_length()) if j >> b & 1]
            self.across(r, j, bits[0] if r < 2 else bits[-1])

    def along_line(self, j, rounds, hops):
        for dist, r, held, moves in self.groups:
            if r not in rounds or dist not in hops:
                continue
            pairs = [
                ((l, a * CORES + c), (l, b * CORES + c))
                for l in range(self.n_layer)
                for a, b in moves
                for c in range(CORES)
            ]
            x = self.tie(self.piece(held, j))
            if dist > 1 and self.ahead is not None:
                x, self.sparse = lax.optimization_barrier((x, self.ahead))
                self.ahead = None
            got = self.permute(x, pairs)
            if (r, j) in self.pieces:
                here = functools.reduce(jnp.logical_or, [self.plane == b for _, b in moves])
                self.later[(r, j)] = (here, got)
            else:
                self.pieces[(r, j)] = got


def prepare_kernel(act, blocks, sparse, mask):
    width, rows = sparse.shape[1:]
    count = blocks.shape[1]
    bits = blocks[0].astype(jnp.float32)
    turned = jnp.concatenate(
        [jnp.broadcast_to(bits[b : b + 1], (width // count, rows)) for b in range(count)], axis=0
    ).astype(jnp.bfloat16)
    sparse[0] = act[0].T * turned
    mask[0] = turned.T


def prepare(activations, active_blocks):
    layers, rows, width = activations.shape
    count = active_blocks.shape[2]

    def block(*shape):
        return pl.BlockSpec((1, *shape), lambda s: (s, 0, 0))

    return pl.pallas_call(
        prepare_kernel,
        grid=(layers,),
        in_specs=[block(rows, width), block(count, rows)],
        out_specs=(block(width, rows), block(rows, width)),
        out_shape=(
            jax.ShapeDtypeStruct((layers, width, rows), jnp.bfloat16),
            jax.ShapeDtypeStruct((layers, rows, width), jnp.bfloat16),
        ),
        cost_estimate=pl.CostEstimate(flops=0, bytes_accessed=6 * layers * rows * width, transcendentals=0),
        compiler_params=pltpu.CompilerParams(vmem_limit_bytes=VMEM_LIMIT),
    )(activations, jnp.swapaxes(active_blocks, 1, 2))


def round_kernel(n_layer, n_tokens, layers, order, first, last, meta, sparse, decoder, *refs):
    refs = list(refs)
    mask = refs.pop(0) if last else None
    acc_in = None if first else refs.pop(0)
    parts = refs[: CORES * n_layer]
    refs = refs[CORES * n_layer :]
    if not first:
        refs.pop(0)
    refs = refs[n_tokens:]
    grad, acc_out, token = refs[:3]
    up_v, sparse_v, dec_v, acc_v, grad_v, feat_v, *sems = refs[3:]
    up_sem, sparse_sem, dec_sem, in_sem, grad_sem, out_sem = sems
    tokens, wide = parts[0].shape[1:]
    both = CORES * wide
    width = decoder.shape[1]
    rows = n_layer * tokens
    plane = jnp.int32(order[0])
    for z in range(1, len(order)):
        plane = jnp.where(meta[0] == z, jnp.int32(order[z]), plane)
    columns = pl.ds(pl.multiple_of(plane * both, both), both)
    token[...] = jnp.zeros_like(token)

    sparse_copies = [
        pltpu.make_async_copy(sparse.at[source], sparse_v.at[source], sparse_sem.at[source])
        for source in range(layers)
    ]
    ups = {}
    for target in range(layers):
        ups[target] = []
        for i, part in enumerate(parts):
            core = meta[1] if i < n_layer else 1 - meta[1]
            at_rows = pl.ds(pl.multiple_of((meta[2] ^ (i % n_layer)) * tokens, tokens), tokens)
            at_cols = pl.ds(pl.multiple_of(target * both + core * wide, wide), wide)
            ups[target].append(
                pltpu.make_async_copy(
                    part.at[target], up_v.at[at_rows, at_cols], up_sem.at[target, i]
                )
            )
    decs = []
    for target in range(layers):
        for source in range(target + 1):
            pair = target * (target + 1) // 2 + source
            decs.append(
                pltpu.make_async_copy(
                    decoder.at[pair, :, columns],
                    dec_v.at[source, :, pl.ds(target * both, both)],
                    dec_sem.at[pair],
                )
            )
    early = layers - 2 if layers > 1 else 0
    sparse_copies[0].start()
    for copy in ups[layers - 1]:
        copy.start()
    for copy in sparse_copies[1:]:
        copy.start()
    for target in reversed(range(early, layers - 1)):
        for copy in ups[target]:
            copy.start()
    for copy in ups[layers - 1]:
        copy.wait()
    for target in reversed(range(early)):
        for copy in ups[target]:
            copy.start()
    for copy in decs:
        copy.start()
    acc_copies = []
    if not first:
        for source in range(layers):
            acc_copies.append(
                pltpu.make_async_copy(acc_in.at[source], acc_v.at[source], in_sem.at[1 + source])
            )
            acc_copies[-1].start()
    if last:
        mask_copy = pltpu.make_async_copy(mask, feat_v, in_sem.at[0])
        mask_copy.start()
    outs = []
    for target in reversed(range(layers)):
        if target < layers - 1:
            for copy in ups[target]:
                copy.wait()
        count = target + 1
        base = target * (target + 1) // 2
        for source in range(count):
            if target == layers - 1:
                sparse_copies[source].wait()
            grad_v[base + source] = jnp.dot(
                sparse_v[source],
                up_v[:, target * both : (target + 1) * both],
                preferred_element_type=jnp.float32,
            ).astype(jnp.bfloat16)
        out = pltpu.make_async_copy(
            grad_v.at[pl.ds(base, count)], grad.at[pl.ds(base, count), :, columns], grad_sem.at[target]
        )
        out.start()
        outs.append(out)
    for copy in decs:
        copy.wait()
    if last:
        mask_copy.wait()
    def transposed_dot(a, b):
        return lax.dot_general(a, b, (((1,), (1,)), ((), ())), preferred_element_type=jnp.float32)

    for low in range(0, layers, 2):
        group = list(range(low, min(low + 2, layers)))
        high = group[-1]
        if not first:
            for source in group:
                acc_copies[source].wait()
        for at in range(0, rows, CHUNK):
            part = pl.ds(at, CHUNK)
            totals = transposed_dot(
                up_v[at : at + CHUNK, high * both :],
                dec_v[low : high + 1, :, high * both :].reshape(len(group) * width, -1),
            )
            for i, source in enumerate(group):
                total = totals[:, i * width : (i + 1) * width]
                if source < high:
                    own = slice(source * both, high * both)
                    total += transposed_dot(up_v[at : at + CHUNK, own], dec_v[source, :, own])
                if not first:
                    total += acc_v[source, part]
                if last:
                    total *= feat_v[source, part].astype(jnp.float32)
                    feat_v[source, part] = total.astype(jnp.bfloat16)
                else:
                    acc_v[source, part] = total
            some = pl.ds(low, len(group))
            out = pltpu.make_async_copy(
                (feat_v if last else acc_v).at[some, part],
                acc_out.at[some, part],
                out_sem.at[low, at // CHUNK],
            )
            out.start()
            outs.append(out)
    for out in outs:
        out.wait()


def run_round(order, meta, tokens, sparse, decoder, mask, acc, grad, mine, theirs, last):
    first = acc is None
    layers, width, rows = sparse.shape
    wide = mine[0].shape[2]
    pairs = decoder.shape[0]
    operands = [meta, sparse, decoder]
    if last:
        operands.append(mask)
    if not first:
        operands.append(acc)
    operands += mine + theirs
    aliases = {}
    if not first:
        aliases[len(operands)] = 0
        operands.append(grad)
    operands += tokens
    any_space = pl.BlockSpec(memory_space=pl.ANY)
    both = CORES * wide
    return pl.pallas_call(
        functools.partial(round_kernel, len(mine), len(tokens), layers, order, first, last),
        out_shape=(
            jax.ShapeDtypeStruct(decoder.shape, jnp.bfloat16),
            jax.ShapeDtypeStruct((layers, rows, width), jnp.bfloat16 if last else jnp.float32),
            jax.ShapeDtypeStruct((8, 128), jnp.float32),
        ),
        in_specs=[pl.BlockSpec(memory_space=pltpu.SMEM)] + [any_space] * (len(operands) - 1),
        out_specs=(any_space, any_space, pl.BlockSpec(memory_space=pltpu.VMEM)),
        scratch_shapes=[
            pltpu.VMEM((rows, layers * both), jnp.bfloat16),
            pltpu.VMEM((layers, width, rows), jnp.bfloat16),
            pltpu.VMEM((layers, width, layers * both), jnp.bfloat16),
            pltpu.VMEM((layers, rows, width), jnp.float32),
            pltpu.VMEM((pairs, width, both), jnp.bfloat16),
            pltpu.VMEM((layers, rows, width), jnp.bfloat16),
            pltpu.SemaphoreType.DMA((layers, CORES * len(mine))),
            pltpu.SemaphoreType.DMA((layers,)),
            pltpu.SemaphoreType.DMA((pairs,)),
            pltpu.SemaphoreType.DMA((1 + layers,)),
            pltpu.SemaphoreType.DMA((layers,)),
            pltpu.SemaphoreType.DMA((layers, rows // CHUNK)),
        ],
        input_output_aliases=aliases,
        cost_estimate=pl.CostEstimate(
            flops=2 * 4 * pairs * width * rows * both, bytes_accessed=20 * 2**20, transcendentals=0
        ),
        compiler_params=pltpu.CompilerParams(vmem_limit_bytes=VMEM_LIMIT),
    )(*operands)


def body(n_layer, n_feat, activations, active_blocks, cotangent, decoder):
    sparse, mask = prepare(activations, active_blocks)
    blocks = Gather(cotangent, sparse, n_layer, n_feat)
    planes = blocks.planes
    end = planes - 1
    core = lax.axis_index("feat") % CORES
    place = jnp.stack([blocks.plane, core, lax.axis_index("layer")]).astype(jnp.int32)
    hops = range(1, planes)
    acc = grad = None
    for r in range(planes):
        if r == 0:
            blocks.straight(0)
            blocks.along_line(0, range(1, planes), hops)
            for near in range(1, min(3, planes)):
                blocks.straight(near)
            blocks.diagonal(0)
            if end > 1:
                blocks.diagonal(1)
            for j in blocks.others:
                blocks.along_line(j, range(2, end), [1])
        else:
            if r + 2 < planes:
                blocks.straight(r + 2)
            for j in blocks.others:
                blocks.along_line(j, range(2, end), [r + 1])
        if r == max(end - 1, 0) and end > 0:
            blocks.diagonal(end)
        mine = [blocks.piece(r, j) for j in range(n_layer)]
        if r == 1 and end > 2:
            held = [(1, j) for j in blocks.others] + [(end, 0)]
            ready = lax.optimization_barrier([blocks.piece(*at) for at in held])
            blocks.pieces.update(zip(held, ready))
            mine = [blocks.piece(r, j) for j in range(n_layer)]
        free = [0] + blocks.singles if r in (0, 1, end) else []
        theirs = [blocks.swap(x if j in free else blocks.tie(x)) for j, x in enumerate(mine)]
        if r == 0:
            soon = [(far, 0) for far in range(1, planes)] + [(1, j) for j in blocks.singles[1:]]
        else:
            soon = [(r + 1, j) for j in blocks.singles[0 if r == end - 1 else 1 :]]
        soon = [at for at in soon if at in blocks.pieces]
        place, *ready = lax.optimization_barrier((place, *[blocks.pieces[at] for at in soon]))
        blocks.pieces.update(zip(soon, ready))
        row = [row[r] for row in blocks.order]
        grad, acc, blocks.token = run_round(
            row, place, blocks.tokens, blocks.sparse, decoder, mask, acc, grad, mine, theirs, r == end
        )
        blocks.tokens = []
    return grad, acc


def solution(mesh):
    in_specs = (
        P(None, None, ("layer", "feat")),
        P(None, None, ("layer", "feat")),
        P(None, "layer", "feat"),
        P(None, ("layer", "feat"), None),
    )
    out_specs = (P(None, ("layer", "feat"), None), P(None, None, ("layer", "feat")))
    work = functools.partial(body, mesh.shape["layer"], mesh.shape["feat"])
    return jax.shard_map(work, mesh=mesh, in_specs=in_specs, out_specs=out_specs, check_vma=False)
```

```python
import functools

import jax
import jax.numpy as jnp
from jax import lax
from jax.experimental import pallas as pl
from jax.experimental.pallas import tpu as pltpu
from jax.sharding import PartitionSpec as P

CORES = 2
VMEM_LIMIT = 60 * 2**20
CHUNK = 256


def plane_order(planes):
    return [
        sorted(range(planes), key=lambda p: (abs(p - z), p != (z ^ 1))) for z in range(planes)
    ]


def line_groups(order):
    groups = {}
    for z, row in enumerate(order):
        for r in range(1, len(row)):
            step = 1 if row[r] > z else -1
            held = order[z + step].index(row[r])
            groups.setdefault((abs(row[r] - z), r, held), []).append((z + step, z))
    return [(*key, groups[key]) for key in sorted(groups)]


class Gather:
    def __init__(self, block, sparse, n_layer, n_feat):
        self.sparse = self.ahead = sparse
        self.n_layer, self.n_feat = n_layer, n_feat
        self.planes = n_feat // CORES
        self.order = plane_order(self.planes)
        self.plane = lax.axis_index("feat") // CORES
        self.groups = line_groups(self.order)
        self.singles = [j for j in range(1, n_layer) if j & (j - 1) == 0]
        self.others = [j for j in range(1, n_layer) if j & (j - 1) != 0]
        self.pieces = {(0, 0): block}
        self.later = {}
        self.token = None
        self.tokens = []

    def piece(self, r, j):
        if (r, j) in self.later:
            here, got = self.later.pop((r, j))
            self.pieces[(r, j)] = jnp.where(here, got, self.pieces[(r, j)])
        return self.pieces[(r, j)]

    def tie(self, x):
        if self.token is None:
            return x
        x, token = lax.optimization_barrier((x, self.token))
        self.tokens.append(token)
        return x

    def permute(self, x, pairs):
        flat = [(l0 * self.n_feat + f0, l1 * self.n_feat + f1) for (l0, f0), (l1, f1) in pairs]
        return lax.ppermute(x, ("layer", "feat"), sorted(flat))

    def swap(self, x):
        every = [(l, f) for l in range(self.n_layer) for f in range(self.n_feat)]
        return self.permute(x, [((l, f), (l, f ^ 1)) for l, f in every])

    def across(self, r, j, bit):
        every = [(l, f) for l in range(self.n_layer) for f in range(self.n_feat)]
        x = self.tie(self.piece(r, j ^ bit))
        self.pieces[(r, j)] = self.permute(x, [((l, f), (l ^ bit, f)) for l, f in every])

    def straight(self, r):
        for j in self.singles:
            self.across(r, j, j)

    def diagonal(self, r):
        for j in self.others:
            bits = [1 << b for b in range(j.bit_length()) if j >> b & 1]
            self.across(r, j, bits[0] if r < 2 else bits[-1])

    def along_line(self, j, rounds, hops):
        for dist, r, held, moves in self.groups:
            if r not in rounds or dist not in hops:
                continue
            pairs = [
                ((l, a * CORES + c), (l, b * CORES + c))
                for l in range(self.n_layer)
                for a, b in moves
                for c in range(CORES)
            ]
            x = self.tie(self.piece(held, j))
            if dist > 1 and self.ahead is not None:
                x, self.sparse = lax.optimization_barrier((x, self.ahead))
                self.ahead = None
            got = self.permute(x, pairs)
            if (r, j) in self.pieces:
                here = functools.reduce(jnp.logical_or, [self.plane == b for _, b in moves])
                self.later[(r, j)] = (here, got)
            else:
                self.pieces[(r, j)] = got


def prepare_kernel(act, blocks, sparse, mask):
    width, rows = sparse.shape[1:]
    count = blocks.shape[1]
    bits = blocks[0].astype(jnp.float32)
    turned = jnp.concatenate(
        [jnp.broadcast_to(bits[b : b + 1], (width // count, rows)) for b in range(count)], axis=0
    ).astype(jnp.bfloat16)
    sparse[0] = act[0].T * turned
    mask[0] = turned.T


def prepare(activations, active_blocks):
    layers, rows, width = activations.shape
    count = active_blocks.shape[2]

    def block(*shape):
        return pl.BlockSpec((1, *shape), lambda s: (s, 0, 0))

    return pl.pallas_call(
        prepare_kernel,
        grid=(layers,),
        in_specs=[block(rows, width), block(count, rows)],
        out_specs=(block(width, rows), block(rows, width)),
        out_shape=(
            jax.ShapeDtypeStruct((layers, width, rows), jnp.bfloat16),
            jax.ShapeDtypeStruct((layers, rows, width), jnp.bfloat16),
        ),
        cost_estimate=pl.CostEstimate(flops=0, bytes_accessed=6 * layers * rows * width, transcendentals=0),
        compiler_params=pltpu.CompilerParams(vmem_limit_bytes=VMEM_LIMIT),
    )(activations, jnp.swapaxes(active_blocks, 1, 2))


def round_kernel(n_layer, n_tokens, layers, order, first, last, meta, sparse, decoder, *refs):
    refs = list(refs)
    mask = refs.pop(0) if last else None
    acc_in = None if first else refs.pop(0)
    parts = refs[: CORES * n_layer]
    refs = refs[CORES * n_layer :]
    if not first:
        refs.pop(0)
    refs = refs[n_tokens:]
    grad, acc_out, token = refs[:3]
    up_v, sparse_v, dec_v, acc_v, grad_v, feat_v, *sems = refs[3:]
    up_sem, sparse_sem, dec_sem, in_sem, grad_sem, out_sem = sems
    tokens, wide = parts[0].shape[1:]
    both = CORES * wide
    width = decoder.shape[1]
    rows = n_layer * tokens
    plane = jnp.int32(order[0])
    for z in range(1, len(order)):
        plane = jnp.where(meta[0] == z, jnp.int32(order[z]), plane)
    columns = pl.ds(pl.multiple_of(plane * both, both), both)
    token[...] = jnp.zeros_like(token)

    sparse_copies = [
        pltpu.make_async_copy(sparse.at[source], sparse_v.at[source], sparse_sem.at[source])
        for source in range(layers)
    ]
    ups = {}
    for target in range(layers):
        ups[target] = []
        for i, part in enumerate(parts):
            core = meta[1] if i < n_layer else 1 - meta[1]
            at_rows = pl.ds(pl.multiple_of((meta[2] ^ (i % n_layer)) * tokens, tokens), tokens)
            at_cols = pl.ds(pl.multiple_of(target * both + core * wide, wide), wide)
            ups[target].append(
                pltpu.make_async_copy(
                    part.at[target], up_v.at[at_rows, at_cols], up_sem.at[target, i]
                )
            )
    decs = []
    for target in range(layers):
        for source in range(target + 1):
            pair = target * (target + 1) // 2 + source
            decs.append(
                pltpu.make_async_copy(
                    decoder.at[pair, :, columns],
                    dec_v.at[source, :, pl.ds(target * both, both)],
                    dec_sem.at[pair],
                )
            )
    early = layers - 2 if layers > 1 else 0
    sparse_copies[0].start()
    for copy in ups[layers - 1]:
        copy.start()
    for copy in sparse_copies[1:]:
        copy.start()
    for target in reversed(range(early, layers - 1)):
        for copy in ups[target]:
            copy.start()
    for copy in ups[layers - 1]:
        copy.wait()
    for target in reversed(range(early)):
        for copy in ups[target]:
            copy.start()
    for copy in decs:
        copy.start()
    acc_copies = []
    if not first:
        for source in range(layers):
            acc_copies.append(
                pltpu.make_async_copy(acc_in.at[source], acc_v.at[source], in_sem.at[1 + source])
            )
            acc_copies[-1].start()
    if last:
        mask_copy = pltpu.make_async_copy(mask, feat_v, in_sem.at[0])
        mask_copy.start()
    outs = []
    for target in reversed(range(layers)):
        if target < layers - 1:
            for copy in ups[target]:
                copy.wait()
        count = target + 1
        base = target * (target + 1) // 2
        for source in range(count):
            if target == layers - 1:
                sparse_copies[source].wait()
            grad_v[base + source] = jnp.dot(
                sparse_v[source],
                up_v[:, target * both : (target + 1) * both],
                preferred_element_type=jnp.float32,
            ).astype(jnp.bfloat16)
        out = pltpu.make_async_copy(
            grad_v.at[pl.ds(base, count)], grad.at[pl.ds(base, count), :, columns], grad_sem.at[target]
        )
        out.start()
        outs.append(out)
    for copy in decs:
        copy.wait()
    if last:
        mask_copy.wait()
    def transposed_dot(a, b):
        return lax.dot_general(a, b, (((1,), (1,)), ((), ())), preferred_element_type=jnp.float32)

    for low in range(0, layers, 2):
        group = list(range(low, min(low + 2, layers)))
        high = group[-1]
        if not first:
            for source in group:
                acc_copies[source].wait()
        for at in range(0, rows, CHUNK):
            part = pl.ds(at, CHUNK)
            totals = transposed_dot(
                up_v[at : at + CHUNK, high * both :],
                dec_v[low : high + 1, :, high * both :].reshape(len(group) * width, -1),
            )
            for i, source in enumerate(group):
                total = totals[:, i * width : (i + 1) * width]
                if source < high:
                    own = slice(source * both, high * both)
                    total += transposed_dot(up_v[at : at + CHUNK, own], dec_v[source, :, own])
                if not first:
                    total += acc_v[source, part]
                if last:
                    total *= feat_v[source, part].astype(jnp.float32)
                    feat_v[source, part] = total.astype(jnp.bfloat16)
                else:
                    acc_v[source, part] = total
            some = pl.ds(low, len(group))
            out = pltpu.make_async_copy(
                (feat_v if last else acc_v).at[some, part],
                acc_out.at[some, part],
                out_sem.at[low, at // CHUNK],
            )
            out.start()
            outs.append(out)
    for out in outs:
        out.wait()


def run_round(order, meta, tokens, sparse, decoder, mask, acc, grad, mine, theirs, last):
    first = acc is None
    layers, width, rows = sparse.shape
    wide = mine[0].shape[2]
    pairs = decoder.shape[0]
    operands = [meta, sparse, decoder]
    if last:
        operands.append(mask)
    if not first:
        operands.append(acc)
    operands += mine + theirs
    aliases = {}
    if not first:
        aliases[len(operands)] = 0
        operands.append(grad)
    operands += tokens
    any_space = pl.BlockSpec(memory_space=pl.ANY)
    both = CORES * wide
    return pl.pallas_call(
        functools.partial(round_kernel, len(mine), len(tokens), layers, order, first, last),
        out_shape=(
            jax.ShapeDtypeStruct(decoder.shape, jnp.bfloat16),
            jax.ShapeDtypeStruct((layers, rows, width), jnp.bfloat16 if last else jnp.float32),
            jax.ShapeDtypeStruct((8, 128), jnp.float32),
        ),
        in_specs=[pl.BlockSpec(memory_space=pltpu.SMEM)] + [any_space] * (len(operands) - 1),
        out_specs=(any_space, any_space, pl.BlockSpec(memory_space=pltpu.VMEM)),
        scratch_shapes=[
            pltpu.VMEM((rows, layers * both), jnp.bfloat16),
            pltpu.VMEM((layers, width, rows), jnp.bfloat16),
            pltpu.VMEM((layers, width, layers * both), jnp.bfloat16),
            pltpu.VMEM((layers, rows, width), jnp.float32),
            pltpu.VMEM((pairs, width, both), jnp.bfloat16),
            pltpu.VMEM((layers, rows, width), jnp.bfloat16),
            pltpu.SemaphoreType.DMA((layers, CORES * len(mine))),
            pltpu.SemaphoreType.DMA((layers,)),
            pltpu.SemaphoreType.DMA((pairs,)),
            pltpu.SemaphoreType.DMA((1 + layers,)),
            pltpu.SemaphoreType.DMA((layers,)),
            pltpu.SemaphoreType.DMA((layers, rows // CHUNK)),
        ],
        input_output_aliases=aliases,
        cost_estimate=pl.CostEstimate(
            flops=2 * 4 * pairs * width * rows * both, bytes_accessed=20 * 2**20, transcendentals=0
        ),
        compiler_params=pltpu.CompilerParams(vmem_limit_bytes=VMEM_LIMIT),
    )(*operands)


def body(n_layer, n_feat, activations, active_blocks, cotangent, decoder):
    sparse, mask = prepare(activations, active_blocks)
    blocks = Gather(cotangent, sparse, n_layer, n_feat)
    planes = blocks.planes
    end = planes - 1
    core = lax.axis_index("feat") % CORES
    place = jnp.stack([blocks.plane, core, lax.axis_index("layer")]).astype(jnp.int32)
    hops = range(1, planes)
    acc = grad = None
    for r in range(planes):
        if r == 0:
            blocks.straight(0)
            blocks.along_line(0, range(1, planes), hops)
            for near in range(1, min(3, planes)):
                blocks.straight(near)
            blocks.diagonal(0)
            if end > 1:
                blocks.diagonal(1)
            for j in blocks.others:
                blocks.along_line(j, range(2, end), [1])
        else:
            if r + 2 < planes:
                blocks.straight(r + 2)
            for j in blocks.others:
                blocks.along_line(j, range(2, end), [r + 1])
        if r == max(end - 1, 0) and end > 0:
            blocks.diagonal(end)
        mine = [blocks.piece(r, j) for j in range(n_layer)]
        if r == 1 and end > 2:
            held = [(1, j) for j in blocks.others] + [(end, 0)]
            ready = lax.optimization_barrier([blocks.piece(*at) for at in held])
            blocks.pieces.update(zip(held, ready))
            mine = [blocks.piece(r, j) for j in range(n_layer)]
        free = [0] + blocks.singles if r in (0, 1, end) else [0]
        theirs = [blocks.swap(x if j in free else blocks.tie(x)) for j, x in enumerate(mine)]
        if r == 0:
            soon = [(far, 0) for far in range(1, planes)] + [(1, j) for j in blocks.singles[1:]]
        else:
            soon = [(r + 1, j) for j in blocks.singles[0 if r == end - 1 else 1 :]]
        soon = [at for at in soon if at in blocks.pieces]
        place, *ready = lax.optimization_barrier((place, *[blocks.pieces[at] for at in soon]))
        blocks.pieces.update(zip(soon, ready))
        row = [row[r] for row in blocks.order]
        grad, acc, blocks.token = run_round(
            row, place, blocks.tokens, blocks.sparse, decoder, mask, acc, grad, mine, theirs, r == end
        )
        blocks.tokens = []
    return grad, acc


def solution(mesh):
    in_specs = (
        P(None, None, ("layer", "feat")),
        P(None, None, ("layer", "feat")),
        P(None, "layer", "feat"),
        P(None, ("layer", "feat"), None),
    )
    out_specs = (P(None, ("layer", "feat"), None), P(None, None, ("layer", "feat")))
    work = functools.partial(body, mesh.shape["layer"], mesh.shape["feat"])
    return jax.shard_map(work, mesh=mesh, in_specs=in_specs, out_specs=out_specs, check_vma=False)
```
